128 devices in a mesh: row: 8 (over z_lo, y), col: 16 (over z_hi, x, core).
Axes of the slice: x: 4, y: 4, z: 4 (z_hi: 2, z_lo: 2; z = z_hi * 2 + z_lo), core: 2. Of those that a mesh axis runs over, the one named last changes fastest.
Arguments:
- activations: bfloat16 [768, 8192], P('col', 'row'), may hold values from -6 to 6
- out_grad: bfloat16 [768, 8192], P('col', 'row'), may hold values from -3 to 3
- w_gate: bfloat16 [8192, 26624], P('row', 'col'), may hold values from -0.0625 to 0.0625
- w_up: bfloat16 [8192, 26624], P('row', 'col'), may hold values from -0.0625 to 0.0625
- w_down: bfloat16 [26624, 8192], P('col', 'row'), may hold values from -0.0390625 to 0.0390625
Outputs:
- input_grad: bfloat16 [768, 8192], P('col', 'row')
- gate_grad: bfloat16 [8192, 26624], P('row', 'col')
- up_grad: bfloat16 [8192, 26624], P('row', 'col')
- down_grad: bfloat16 [26624, 8192], P('col', 'row')
The draws below stay inside these ranges and needn't reach their ends.
All inputs are finite; a program needn't handle non-finite values.
Results may differ from the reference program's by a relative error of at most 0.005.
Values may be sent and summed in bfloat16 or wider, within the bound.
A program may use at most 128 MiB of HBM per device.

```python
import jax
import jax.numpy as jnp

D = 8192
H = 26624
TOKENS = 768


def levels(rng, dims, cuts, low, high):
    level = 1.0
    for position, parts in cuts:
        steps = jax.random.uniform(jax.random.fold_in(jax.random.fold_in(rng, 6), position), (parts,), jnp.float32, low / len(cuts), high / len(cuts))
        level = level * jnp.repeat(jnp.exp(steps), dims[position] // parts).reshape((-1,) + (1,) * (len(dims) - 1 - position))
    return level


def noise(key, extent, spread, most, split=(), dtype=jnp.bfloat16):
    result = spread * jax.random.normal(key, extent, jnp.float32)
    if split:
        result = result * levels(key, extent, split, -0.22, 0.18)
    return jnp.clip(result, -most, most).astype(dtype)


def setup_inputs(seed: int = 0) -> dict:
    splits = jax.random.split(jax.random.key(seed), 6)
    return {
        "activations": noise(splits[0], (TOKENS, D), 1.0, 6.0, ((0, 16), (1, 8))),
        "out_grad": noise(splits[1], (TOKENS, D), (TOKENS ** -0.25), 3.0, ((0, 16), (1, 8))),
        "w_gate": noise(splits[2], (D, H), D ** -0.5, 0.0625, ((0, 8), (1, 16))),
        "w_up": noise(splits[3], (D, H), D ** -0.5, 0.0625, ((0, 8), (1, 16))),
        "w_down": noise(splits[4], (H, D), H ** -0.5, 0.0390625, ((0, 16), (1, 8))),
    }


def reference(activations, out_grad, w_gate, w_up, w_down):
    gate = jnp.dot(activations, w_gate, preferred_element_type=jnp.float32)
    upper = jnp.dot(activations, w_up, preferred_element_type=jnp.float32)
    hidden_grad = jnp.dot(out_grad, w_down.T, preferred_element_type=jnp.float32)
    sig = jax.nn.sigmoid(gate)
    act = gate * sig
    hidden = (act * upper).astype(jnp.bfloat16)
    gate_delta = (hidden_grad * upper * sig * (1.0 + gate * (1.0 - sig))).astype(jnp.bfloat16)
    up_delta = (hidden_grad * act).astype(jnp.bfloat16)
    gate_grad = jnp.dot(activations.T, gate_delta, preferred_element_type=jnp.float32).astype(jnp.bfloat16)
    up_grad = jnp.dot(activations.T, up_delta, preferred_element_type=jnp.float32).astype(jnp.bfloat16)
    down_grad = jnp.dot(hidden.T, out_grad, preferred_element_type=jnp.float32).astype(jnp.bfloat16)
    input_grad = (jnp.dot(gate_delta, w_gate.T, preferred_element_type=jnp.float32)
                  + jnp.dot(up_delta, w_up.T, preferred_element_type=jnp.float32)).astype(jnp.bfloat16)
    return input_grad, gate_grad, up_grad, down_grad
```

```python
import functools

import jax
import jax.numpy as jnp
from jax import lax
from jax.experimental import pallas as pl
from jax.experimental.pallas import tpu as pltpu
from jax.sharding import PartitionSpec as P

F32 = jnp.float32
BF16 = jnp.bfloat16
MESH = pl.DeviceIdType.MESH

CHUNKS = 6
CHUNK = 128
OWN = 16
D_LOCAL = 1024
H_LOCAL = 1664
TOKENS = 768
BLOCK = 48
SLOT = 192
WIDTH_A = 896
WIDTH_B = H_LOCAL - WIDTH_A
STAGES = 4


def dot_nn(a, b):
    return jnp.dot(a, b, preferred_element_type=F32)


def dot_nt(a, b):
    return lax.dot_general(a, b, (((1,), (1,)), ((), ())), preferred_element_type=F32)


def dot_tn(a, b):
    return lax.dot_general(a, b, (((0,), (0,)), ((), ())), preferred_element_type=F32)


def swiglu_back(gate, upper, hidden_grad):
    sig = jax.nn.sigmoid(gate)
    act = gate * sig
    hidden = (act * upper).astype(BF16)
    gate_delta = (hidden_grad * upper * sig * (1.0 + gate * (1.0 - sig))).astype(BF16)
    up_delta = (hidden_grad * act).astype(BF16)
    return hidden, gate_delta, up_delta


def exchange_kernel(
    act_in, grad_in, wg_in, wu_in, wd_in,
    tokens_out, delta_out, input_grad_out,
    wg, wu, wd, tok, part_a, part_b,
    send_a1, recv_a1, send_a2, recv_a2,
    send_b1, recv_b1, send_b2, recv_b2,
    delta_a, delta_b, igrad, core_recv, x_recv, z_recv,
    load_sem, gather_s, gather_r,
    a1_s, a1_r, a2_s, a2_r, b1_s, b1_r, b2_s, b2_r,
    ga1_s, ga1_r, ga2_s, ga2_r, gb1_s, gb1_r, gb2_s, gb2_r,
    core_s, core_r, x_s, x_r, z_s, z_r, out_sem,
):
    row = lax.axis_index("row")
    col = lax.axis_index("col")
    y = lax.rem(row, 4)
    zl = lax.div(row, 4)
    zh = lax.div(col, 8)
    x = lax.rem(lax.div(col, 2), 4)
    core = lax.rem(col, 2)

    def at_y(dist):
        return (zl * 4 + lax.rem(y + dist, 4), col)

    def at_x(dist):
        return (row, zh * 8 + lax.rem(x + dist, 4) * 2 + core)

    z_pair = ((1 - zl) * 4 + y, col)
    zh_pair = (row, (1 - zh) * 8 + x * 2 + core)
    sibling = (row, zh * 8 + x * 2 + 1 - core)
    partners = [at_y(1), at_y(2), at_y(3), z_pair, at_x(1), at_x(2), at_x(3), zh_pair, sibling]

    def remote(src, dst, send, recv, device):
        return pltpu.make_async_remote_copy(
            src_ref=src, dst_ref=dst, send_sem=send, recv_sem=recv,
            device_id=device, device_id_type=MESH,
        )

    own_row = core * 96 + zh * BLOCK
    loads = [
        pltpu.make_async_copy(act_in, tok.at[0, pl.ds(own_row, BLOCK)], load_sem.at[0]),
        pltpu.make_async_copy(grad_in, tok.at[1, pl.ds(own_row, BLOCK)], load_sem.at[1]),
        pltpu.make_async_copy(wg_in, wg, load_sem.at[2]),
        pltpu.make_async_copy(wu_in, wu, load_sem.at[3]),
        pltpu.make_async_copy(wd_in, wd, load_sem.at[4]),
    ]
    for load in loads:
        load.start()

    barrier = pltpu.get_barrier_semaphore()
    for device in partners:
        pl.semaphore_signal(barrier, inc=1, device_id=device, device_id_type=MESH)
    pl.semaphore_wait(barrier, len(partners))

    def blk(slot, core_, zh_):
        return tok.at[:, pl.ds(slot * SLOT + core_ * 96 + zh_ * BLOCK, BLOCK)]

    slot_dist = (0, 1, 3, 2)
    slot_at = (0, 2, 1, 3)

    def to_zh():
        return remote(blk(0, core, zh), blk(0, core, zh), gather_s.at[0], gather_r.at[0], zh_pair)

    def to_sibling(slot, which):
        zh_ = zh if which == 0 else 1 - zh
        sem = 1 + which if slot == 0 else 3 + 4 * (slot - 1) + 2 + which
        return remote(blk(slot, core, zh_), blk(slot, core, zh_), gather_s.at[sem], gather_r.at[sem], sibling)

    def to_x(slot, which):
        zh_ = zh if which == 0 else 1 - zh
        sem = 3 + 4 * (slot - 1) + which
        return remote(
            blk(0, core, zh_), blk(slot, core, zh_), gather_s.at[sem], gather_r.at[sem],
            at_x(slot_dist[slot_at[slot]]),
        )

    loads[0].wait()
    loads[1].wait()
    to_zh().start()
    to_sibling(0, 0).start()
    for slot in (1, 2, 3):
        to_x(slot, 0).start()
    to_zh().wait_recv()
    to_sibling(0, 1).start()
    for slot in (1, 2, 3):
        to_x(slot, 1).start()
    for which in (0, 1):
        to_sibling(0, which).wait_recv()
    for load in loads[2:]:
        load.wait()

    def slot_arrives(slot):
        for which in (0, 1):
            to_x(slot, which).wait_recv()
            to_sibling(slot, which).start()
        for which in (0, 1):
            to_sibling(slot, which).wait_recv()

    plane = pl.ds(64 * zl, 64)
    other_plane = pl.ds(64 * (1 - zl), 64)

    def copy_a1(c):
        return remote(send_a1.at[c], recv_a1.at[c], a1_s.at[c], a1_r.at[c], z_pair)

    def copy_a2(c, d):
        src = send_a2.at[c, :, pl.ds(OWN * lax.rem(y + d, 4), OWN)]
        return remote(src, recv_a2.at[c, d - 1], a2_s.at[c, d - 1], a2_r.at[c, d - 1], at_y(d))

    def copy_b1(c, d):
        src = send_b1.at[c, :, pl.ds(32 * lax.rem(y + d, 4), 32)]
        return remote(src, recv_b1.at[c, d - 1], b1_s.at[c, d - 1], b1_r.at[c, d - 1], at_y(d))

    def copy_b2(c):
        return remote(send_b2.at[c], recv_b2.at[c], b2_s.at[c], b2_r.at[c], z_pair)

    def gather_a1(c, d):
        src = delta_a.at[:, pl.ds(c * CHUNK + 64 * zl + OWN * y, OWN)]
        return remote(src, src, ga1_s.at[c, d - 1], ga1_r.at[c, d - 1], at_y(d))

    def gather_a2(c):
        src = delta_a.at[:, pl.ds(c * CHUNK + 64 * zl, 64)]
        return remote(src, src, ga2_s.at[c], ga2_r.at[c], z_pair)

    def gather_b1(c):
        src = delta_b.at[:, pl.ds(c * CHUNK + 32 * y + OWN * zl, OWN)]
        return remote(src, src, gb1_s.at[c], gb1_r.at[c], z_pair)

    def gather_b2(c, d):
        src = delta_b.at[:, pl.ds(c * CHUNK + 32 * y, 32)]
        return remote(src, src, gb2_s.at[c, d - 1], gb2_r.at[c, d - 1], at_y(d))

    def out_copies(c):
        rows = pl.ds(c * CHUNK, CHUNK)
        return (
            pltpu.make_async_copy(delta_a.at[:, rows], delta_out.at[:, rows, pl.ds(0, WIDTH_A)], out_sem.at[0, c]),
            pltpu.make_async_copy(delta_b.at[:, rows], delta_out.at[:, rows, pl.ds(WIDTH_A, WIDTH_B)], out_sem.at[1, c]),
        )

    tokens_copy = pltpu.make_async_copy(tok, tokens_out, load_sem.at[0])

    def stage0(c):
        p = lax.rem(c, 2)
        rows = pl.ds(c * CHUNK, CHUNK)
        act, grad = tok[0, rows, :], tok[1, rows, :]
        part_a[p, 0] = dot_nn(act, wg[:, :WIDTH_A])
        part_a[p, 1] = dot_nn(act, wu[:, :WIDTH_A])
        part_a[p, 2] = dot_nt(grad, wd[:WIDTH_A, :])
        for i in range(3):
            send_a1[c, i] = part_a[p, i, other_plane, :].astype(BF16)
        copy_a1(c).start()
        part_b[p, 0] = dot_nn(act, wg[:, WIDTH_A:])
        part_b[p, 1] = dot_nn(act, wu[:, WIDTH_A:])
        part_b[p, 2] = dot_nt(grad, wd[WIDTH_A:, :])
        for i in range(3):
            send_b1[c, i] = part_b[p, i].astype(BF16)
        for d in (2, 1, 3):
            copy_b1(c, d).start()

    def stage1(c):
        p = lax.rem(c, 2)
        copy_a1(c).wait_recv()
        for i in range(3):
            total = part_a[p, i, plane, :] + recv_a1[c, i].astype(F32)
            part_a[p, i, plane, :] = total
            send_a2[c, i] = total.astype(BF16)
        for d in (2, 1, 3):
            copy_a2(c, d).start()
        for d in (1, 2, 3):
            copy_b1(c, d).wait_recv()
        mine = pl.ds(32 * y, 32)
        for i in range(3):
            total = part_b[p, i, mine, :]
            for d in range(3):
                total = total + recv_b1[c, d, i].astype(F32)
            part_b[p, i, mine, :] = total
            send_b2[c, i] = part_b[p, i, pl.ds(32 * y + OWN * (1 - zl), OWN), :].astype(BF16)
        copy_b2(c).start()

    def stage2(c):
        p = lax.rem(c, 2)
        for d in (1, 2, 3):
            copy_a2(c, d).wait_recv()
        own = pl.ds(64 * zl + OWN * y, OWN)
        sums = []
        for i in range(3):
            total = part_a[p, i, own, :]
            for d in range(3):
                total = total + recv_a2[c, d, i].astype(F32)
            sums.append(total)
        for i, value in enumerate(swiglu_back(*sums)):
            delta_a[i, pl.ds(c * CHUNK + 64 * zl + OWN * y, OWN), :] = value
        for d in (2, 1, 3):
            gather_a1(c, d).start()
        copy_b2(c).wait_recv()
        own = pl.ds(32 * y + OWN * zl, OWN)
        sums = [part_b[p, i, own, :] + recv_b2[c, i].astype(F32) for i in range(3)]
        for i, value in enumerate(swiglu_back(*sums)):
            delta_b[i, pl.ds(c * CHUNK + 32 * y + OWN * zl, OWN), :] = value
        gather_b1(c).start()

    def recv_rows(ref, start, size, send, recv, device):
        view = ref.at[:, pl.ds(start, size)]
        return remote(view, view, send, recv, device)

    def stage3(c):
        for d in (1, 2, 3):
            start = c * CHUNK + 64 * zl + OWN * lax.rem(y + 4 - d, 4)
            recv_rows(delta_a, start, OWN, ga1_s.at[c, d - 1], ga1_r.at[c, d - 1], at_y(d)).wait_recv()
        gather_a2(c).start()
        start = c * CHUNK + 32 * y + OWN * (1 - zl)
        recv_rows(delta_b, start, OWN, gb1_s.at[c], gb1_r.at[c], z_pair).wait_recv()
        for d in (2, 1, 3):
            gather_b2(c, d).start()

    def stage4(c):
        recv_rows(delta_a, c * CHUNK + 64 * (1 - zl), 64, ga2_s.at[c], ga2_r.at[c], z_pair).wait_recv()
        for d in (1, 2, 3):
            start = c * CHUNK + 32 * lax.rem(y + 4 - d, 4)
            recv_rows(delta_b, start, 32, gb2_s.at[c, d - 1], gb2_r.at[c, d - 1], at_y(d)).wait_recv()
        for copy in out_copies(c):
            copy.start()
        rows = pl.ds(c * CHUNK, CHUNK)
        igrad[rows, :] = dot_nt(delta_a[1, rows, :], wg[:, :WIDTH_A])
        igrad[rows, :] += dot_nt(delta_b[1, rows, :], wg[:, WIDTH_A:])
        igrad[rows, :] += dot_nt(delta_a[2, rows, :], wu[:, :WIDTH_A])
        igrad[rows, :] += dot_nt(delta_b[2, rows, :], wu[:, WIDTH_A:])

    def core_rows(slot, core_):
        return pl.ds(slot * SLOT + core_ * 96, 96)

    def core_copy(slot):
        return remote(
            igrad.at[core_rows(slot, 1 - core)], core_recv.at[slot], core_s.at[slot], core_r.at[slot], sibling
        )

    def x_copy(slot):
        return remote(
            igrad.at[core_rows(slot, core)], x_recv.at[slot - 1], x_s.at[slot - 1], x_r.at[slot - 1],
            at_x(slot_dist[slot]),
        )

    def z_copy():
        return remote(
            igrad.at[pl.ds(core * 96 + (1 - zh) * BLOCK, BLOCK)], z_recv, z_s.at[0], z_r.at[0], zh_pair
        )

    def sum_core(slot):
        core_copy(slot).wait_recv()
        rows = core_rows(slot, core)
        igrad[rows, :] = igrad[rows, :] + core_recv[slot]
        if slot:
            x_copy(slot).start()

    last_chunk = (1, 2, 4, 5)

    @pl.loop(0, CHUNKS + STAGES)
    def _(t):
        @pl.when(t >= 4)
        def _():
            stage4(t - 4)

        for slot in range(4):
            @pl.when(t == last_chunk[slot] + 4)
            def _():
                core_copy(slot).start()

        @pl.when((t >= 3) & (t < CHUNKS + 3))
        def _():
            stage3(t - 3)

        @pl.when((t >= 2) & (t < CHUNKS + 2))
        def _():
            stage2(t - 2)

        @pl.when((t >= 1) & (t < CHUNKS + 1))
        def _():
            stage1(t - 1)

        for slot in (1, 2, 3):
            @pl.when(t == slot)
            def _():
                slot_arrives(slot)

        @pl.when(t < CHUNKS)
        def _():
            stage0(t)

        @pl.when(t == 3)
        def _():
            tokens_copy.start()

        for slot in range(3):
            @pl.when(t == last_chunk[slot] + 5)
            def _():
                sum_core(slot)

    sum_core(3)
    rows = core_rows(0, core)
    for slot in (1, 2, 3):
        x_copy(slot).wait_recv()
        igrad[rows, :] = igrad[rows, :] + x_recv[slot - 1]
    z_copy().start()
    z_copy().wait_recv()
    mine = pl.ds(own_row, BLOCK)
    input_grad_out[...] = (igrad[mine, :] + z_recv[...]).astype(BF16)

    to_zh().wait_send()
    for which in (0, 1):
        for slot in (1, 2, 3):
            to_x(slot, which).wait_send()
        for slot in range(4):
            to_sibling(slot, which).wait_send()

    @pl.loop(0, CHUNKS)
    def _(c):
        copy_a1(c).wait_send()
        copy_b2(c).wait_send()
        gather_a2(c).wait_send()
        gather_b1(c).wait_send()
        for d in (1, 2, 3):
            copy_a2(c, d).wait_send()
            copy_b1(c, d).wait_send()
            gather_a1(c, d).wait_send()
            gather_b2(c, d).wait_send()
        for copy in out_copies(c):
            copy.wait()

    for slot in range(4):
        core_copy(slot).wait_send()
    for slot in (1, 2, 3):
        x_copy(slot).wait_send()
    z_copy().wait_send()
    tokens_copy.wait()


def exchange(activations, out_grad, w_gate, w_up, w_down):
    dma = pltpu.SemaphoreType.DMA
    any_spec = pl.BlockSpec(memory_space=pl.ANY)
    n = CHUNKS
    return pl.pallas_call(
        exchange_kernel,
        out_shape=[
            jax.ShapeDtypeStruct((2, TOKENS, D_LOCAL), BF16),
            jax.ShapeDtypeStruct((3, TOKENS, H_LOCAL), BF16),
            jax.ShapeDtypeStruct((BLOCK, D_LOCAL), BF16),
        ],
        in_specs=[any_spec] * 5,
        out_specs=[any_spec, any_spec, pl.BlockSpec(memory_space=pltpu.VMEM)],
        scratch_shapes=[
            pltpu.VMEM((D_LOCAL, H_LOCAL), BF16),
            pltpu.VMEM((D_LOCAL, H_LOCAL), BF16),
            pltpu.VMEM((H_LOCAL, D_LOCAL), BF16),
            pltpu.VMEM((2, TOKENS, D_LOCAL), BF16),
            pltpu.VMEM((2, 3, CHUNK, WIDTH_A), F32),
            pltpu.VMEM((2, 3, CHUNK, WIDTH_B), F32),
            pltpu.VMEM((n, 3, 64, WIDTH_A), BF16),
            pltpu.VMEM((n, 3, 64, WIDTH_A), BF16),
            pltpu.VMEM((n, 3, 64, WIDTH_A), BF16),
            pltpu.VMEM((n, 3, 3, OWN, WIDTH_A), BF16),
            pltpu.VMEM((n, 3, CHUNK, WIDTH_B), BF16),
            pltpu.VMEM((n, 3, 3, 32, WIDTH_B), BF16),
            pltpu.VMEM((n, 3, OWN, WIDTH_B), BF16),
            pltpu.VMEM((n, 3, OWN, WIDTH_B), BF16),
            pltpu.VMEM((3, TOKENS, WIDTH_A), BF16),
            pltpu.VMEM((3, TOKENS, WIDTH_B), BF16),
            pltpu.VMEM((TOKENS, D_LOCAL), F32),
            pltpu.VMEM((4, 96, D_LOCAL), F32),
            pltpu.VMEM((3, 96, D_LOCAL), F32),
            pltpu.VMEM((BLOCK, D_LOCAL), F32),
            dma((5,)), dma((15,)), dma((15,)),
            dma((n,)), dma((n,)), dma((n, 3)), dma((n, 3)),
            dma((n, 3)), dma((n, 3)), dma((n,)), dma((n,)),
            dma((n, 3)), dma((n, 3)), dma((n,)), dma((n,)),
            dma((n,)), dma((n,)), dma((n, 3)), dma((n, 3)),
            dma((4,)), dma((4,)), dma((3,)), dma((3,)), dma((1,)), dma((1,)),
            dma((2, n)),
        ],
        compiler_params=pltpu.CompilerParams(
            collective_id=0, has_side_effects=True, vmem_limit_bytes=60 * 2**20
        ),
        cost_estimate=pl.CostEstimate(
            flops=10 * TOKENS * D_LOCAL * H_LOCAL, bytes_accessed=22 * 2**20, transcendentals=0
        ),
        name="exchange",
    )(activations, out_grad, w_gate, w_up, w_down)


def weights_kernel(
    tok_in, delta_in, gate_out, up_out, down_out,
    tok, delta, gate, up, down, in_sem, out_sem,
):
    loads = [
        pltpu.make_async_copy(tok_in.at[0], tok.at[0], in_sem.at[0]),
        pltpu.make_async_copy(delta_in.at[1], delta.at[1], in_sem.at[1]),
        pltpu.make_async_copy(delta_in.at[2], delta.at[2], in_sem.at[2]),
        pltpu.make_async_copy(delta_in.at[0], delta.at[0], in_sem.at[3]),
        pltpu.make_async_copy(tok_in.at[1], tok.at[1], in_sem.at[4]),
    ]
    for load in loads:
        load.start()
    stores = []

    def store(src, dst, start, size):
        copy = pltpu.make_async_copy(
            src.at[pl.ds(start, size)], dst.at[pl.ds(start, size)], out_sem.at[len(stores)]
        )
        copy.start()
        stores.append(copy)

    loads[0].wait()
    for load, i, buf, out in ((loads[1], 1, gate, gate_out), (loads[2], 2, up, up_out)):
        load.wait()
        for m in range(0, D_LOCAL, 256):
            buf[m : m + 256, :] = dot_tn(tok[0, :, m : m + 256], delta[i]).astype(BF16)
            store(buf, out, m, 256)
    loads[3].wait()
    loads[4].wait()
    for m in range(0, H_LOCAL, 256):
        size = min(256, H_LOCAL - m)
        down[m : m + size, :] = dot_tn(delta[0, :, m : m + size], tok[1]).astype(BF16)
        store(down, down_out, m, size)
    for copy in stores:
        copy.wait()


def weight_grads(tokens, deltas):
    any_spec = pl.BlockSpec(memory_space=pl.ANY)
    shapes = [(D_LOCAL, H_LOCAL), (D_LOCAL, H_LOCAL), (H_LOCAL, D_LOCAL)]
    return pl.pallas_call(
        weights_kernel,
        out_shape=[jax.ShapeDtypeStruct(s, BF16) for s in shapes],
        in_specs=[any_spec] * 2,
        out_specs=[any_spec] * 3,
        scratch_shapes=[
            pltpu.VMEM((2, TOKENS, D_LOCAL), BF16),
            pltpu.VMEM((3, TOKENS, H_LOCAL), BF16),
            *[pltpu.VMEM(s, BF16) for s in shapes],
            pltpu.SemaphoreType.DMA((5,)),
            pltpu.SemaphoreType.DMA((15,)),
        ],
        compiler_params=pltpu.CompilerParams(vmem_limit_bytes=56 * 2**20),
        cost_estimate=pl.CostEstimate(
            flops=6 * TOKENS * D_LOCAL * H_LOCAL, bytes_accessed=22 * 2**20, transcendentals=0
        ),
        name="weight_grads",
    )(tokens, deltas)


def per_device(activations, out_grad, w_gate, w_up, w_down):
    tokens, deltas, input_grad = exchange(activations, out_grad, w_gate, w_up, w_down)
    gate_grad, up_grad, down_grad = weight_grads(tokens, deltas)
    return input_grad, gate_grad, up_grad, down_grad


def solution(mesh):
    placed = (P("col", "row"), P("col", "row"), P("row", "col"), P("row", "col"), P("col", "row"))
    return jax.shard_map(
        per_device,
        mesh=mesh,
        in_specs=placed,
        out_specs=(P("col", "row"), P("row", "col"), P("row", "col"), P("col", "row")),
        check_vma=False,
    )
```

```python
import functools

import jax
import jax.numpy as jnp
from jax import lax
from jax.experimental import pallas as pl
from jax.experimental.pallas import tpu as pltpu
from jax.sharding import PartitionSpec as P

F32 = jnp.float32
BF16 = jnp.bfloat16
MESH = pl.DeviceIdType.MESH

CHUNKS = 6
CHUNK = 128
OWN = 16
SLOTS = 4
D_LOCAL = 1024
H_LOCAL = 1664
TOKENS = 768
BLOCK = 48
UNIT = 96
WIDTH_A = 640
HALF_A = 384
WIDTH_B = H_LOCAL - WIDTH_A


def dot_nn(a, b):
    return jnp.dot(a, b, preferred_element_type=F32)


def dot_nt(a, b):
    return lax.dot_general(a, b, (((1,), (1,)), ((), ())), preferred_element_type=F32)


def dot_tn(a, b):
    return lax.dot_general(a, b, (((0,), (0,)), ((), ())), preferred_element_type=F32)


def swiglu_back(gate, upper, hidden_grad):
    sig = jax.nn.sigmoid(gate)
    act = gate * sig
    hidden = (act * upper).astype(BF16)
    gate_delta = (hidden_grad * upper * sig * (1.0 + gate * (1.0 - sig))).astype(BF16)
    up_delta = (hidden_grad * act).astype(BF16)
    return hidden, gate_delta, up_delta


def exchange_kernel(
    act_in, grad_in, wg_in, wu_in, wd_in,
    tokens_out, delta_out, near_out, other_out, far_out,
    wg, wu, wd, tok, part_a, part_b,
    send_az, recv_az, send_ay, recv_af, recv_as, recv_ay,
    send_by, recv_bu, recv_by, send_bz, recv_bz,
    delta_a, delta_b, igrad, core_recv, x_recv,
    load_sem, zh_s, zh_r, sib_s, sib_r, tokx_s, tokx_r,
    az_s, az_r, bz_s, bz_r, gaz_s, gaz_r, gbz_s, gbz_r,
    ay_s, ay_r, by_s, by_r, gay_s, gay_r, gby_s, gby_r,
    core_s, core_r, x_s, x_r, out_sem,
):
    row = lax.axis_index("row")
    col = lax.axis_index("col")
    y = lax.rem(row, 4)
    zl = lax.div(row, 4)
    zh = lax.div(col, 8)
    x = lax.rem(lax.div(col, 2), 4)
    core = lax.rem(col, 2)
    y_next, y_prev, y_far = lax.rem(y + 1, 4), lax.rem(y + 3, 4), lax.rem(y + 2, 4)

    def at_x(dist):
        return (row, zh * 8 + lax.rem(x + dist, 4) * 2 + core)

    up_y = (zl * 4 + y_next, col)
    down_y = (zl * 4 + y_prev, col)
    z_pair = ((1 - zl) * 4 + y, col)
    zh_pair = (row, (1 - zh) * 8 + x * 2 + core)
    sibling = (row, zh * 8 + x * 2 + 1 - core)
    partners = [up_y, down_y, z_pair, at_x(1), at_x(2), at_x(3), zh_pair, sibling]

    def remote(src, dst, send, recv, device):
        return pltpu.make_async_remote_copy(
            src_ref=src, dst_ref=dst, send_sem=send, recv_sem=recv,
            device_id=device, device_id_type=MESH,
        )

    unit_dist = (0, 1, 3, 2, 1, 3, 2, 0)
    to_unit = {(0, 3): 1, (0, 1): 2, (0, 2): 3, (1, 3): 4, (1, 1): 5, (1, 2): 6}

    def blk(unit, core_):
        return tok.at[:, pl.ds(unit * UNIT + core_ * BLOCK, BLOCK)]

    def to_zh():
        return remote(blk(0, core), blk(7, core), zh_s.at[0], zh_r.at[0], zh_pair)

    def to_sibling(unit):
        return remote(blk(unit, core), blk(unit, core), sib_s.at[unit], sib_r.at[unit], sibling)

    def to_x(other, dist):
        unit = to_unit[other, dist]
        return remote(blk(7 * other, core), blk(unit, core), tokx_s.at[unit - 1], tokx_r.at[unit - 1], at_x(dist))

    def pass_on(unit):
        if unit == 7:
            to_zh().wait_recv()
        else:
            view = blk(unit, core)
            remote(view, view, tokx_s.at[unit - 1], tokx_r.at[unit - 1], at_x(unit_dist[unit])).wait_recv()
        to_sibling(unit).start()

    own = pl.ds(core * BLOCK, BLOCK)
    loads = [
        pltpu.make_async_copy(act_in, tok.at[0, own], load_sem.at[0]),
        pltpu.make_async_copy(grad_in, tok.at[1, own], load_sem.at[1]),
        pltpu.make_async_copy(wg_in, wg, load_sem.at[2]),
        pltpu.make_async_copy(wu_in, wu, load_sem.at[3]),
        pltpu.make_async_copy(wd_in, wd, load_sem.at[4]),
    ]
    for load in loads:
        load.start()

    barrier = pltpu.get_barrier_semaphore()
    for device in partners:
        pl.semaphore_signal(barrier, inc=1, device_id=device, device_id_type=MESH)
    pl.semaphore_wait(barrier, len(partners))

    loads[0].wait()
    loads[1].wait()
    to_x(0, 3).start()
    to_x(0, 1).start()
    to_sibling(0).start()
    to_zh().start()
    to_x(0, 2).start()
    pass_on(1)
    for load in loads[2:]:
        load.wait()
    to_sibling(0).wait_recv()
    to_sibling(1).wait_recv()

    def rows_a(c, y_):
        return pl.ds(c * CHUNK + 64 * zl + OWN * y_, OWN)

    def rows_b(c, y_, first, size):
        return pl.ds(c * CHUNK + 32 * y_ + first, size)

    first_a, second_a = pl.ds(0, HALF_A), pl.ds(HALF_A, WIDTH_A - HALF_A)

    def send_az_copy(c):
        return remote(send_az.at[c], recv_az.at[c], az_s.at[c], az_r.at[c], z_pair)

    def send_bz_copy(c):
        return remote(send_bz.at[c], recv_bz.at[c], bz_s.at[c], bz_r.at[c], z_pair)

    def ay(c, k):
        def src(y_, cols):
            return send_ay.at[c, :, pl.ds(OWN * y_, OWN), cols]

        sem = (ay_s.at[c, k], ay_r.at[c, k])
        if k == 0:
            return remote(src(y_far, first_a), recv_af.at[c], *sem, up_y)
        if k == 1:
            return remote(src(y_far, second_a), recv_as.at[c], *sem, down_y)
        if k == 2:
            return remote(src(y_next, second_a), recv_ay.at[c, 0, :, :, second_a], *sem, up_y)
        if k == 3:
            return remote(src(y_prev, first_a), recv_ay.at[c, 1, :, :, first_a], *sem, down_y)
        if k == 4:
            return remote(src(y_next, first_a), recv_ay.at[c, 0, :, :, first_a], *sem, up_y)
        return remote(src(y_prev, second_a), recv_ay.at[c, 1, :, :, second_a], *sem, down_y)

    def by(c, k):
        def src(y_, half):
            return send_by.at[c, :, pl.ds(32 * y_ + OWN * half, OWN)]

        def dst(side, half):
            return recv_by.at[c, side, :, pl.ds(OWN * half, OWN)]

        sem = (by_s.at[c, k], by_r.at[c, k])
        if k == 0:
            return remote(src(y_far, 0), recv_bu.at[c, 0], *sem, up_y)
        if k == 1:
            return remote(src(y_far, 1), recv_bu.at[c, 1], *sem, down_y)
        if k == 2:
            return remote(src(y_next, 1), dst(0, 1), *sem, up_y)
        if k == 3:
            return remote(src(y_prev, 0), dst(1, 0), *sem, down_y)
        if k == 4:
            return remote(src(y_next, 0), dst(0, 0), *sem, up_y)
        return remote(src(y_prev, 1), dst(1, 1), *sem, down_y)

    def same(view, send, recv, device):
        return remote(view, view, send, recv, device)

    def gather_az(c, zl_):
        view = delta_a.at[:, pl.ds(c * CHUNK + 64 * zl_, 64)]
        return same(view, gaz_s.at[c], gaz_r.at[c], z_pair)

    def gather_bz(c, zl_):
        return same(delta_b.at[:, rows_b(c, y, OWN * zl_, OWN)], gbz_s.at[c], gbz_r.at[c], z_pair)

    def gather_ay(c, k, y_):
        sem = (gay_s.at[c, k], gay_r.at[c, k])
        rows = rows_a(c, y_)
        view = (delta_a.at[:, rows], delta_a.at[:, rows],
                delta_a.at[:, rows, second_a], delta_a.at[:, rows, first_a])[k]
        return same(view, *sem, down_y if k % 2 else up_y)

    def gather_by(c, k, y_):
        sem = (gby_s.at[c, k], gby_r.at[c, k])
        rows = (rows_b(c, y_, 0, 32), rows_b(c, y_, 0, 32), rows_b(c, y_, OWN, OWN), rows_b(c, y_, 0, OWN))[k]
        return same(delta_b.at[:, rows], *sem, down_y if k % 2 else up_y)

    def out_copies(c):
        rows = pl.ds(c * CHUNK, CHUNK)
        return (
            pltpu.make_async_copy(delta_a.at[:, rows], delta_out.at[:, rows, pl.ds(0, WIDTH_A)], out_sem.at[0, c]),
            pltpu.make_async_copy(delta_b.at[:, rows], delta_out.at[:, rows, pl.ds(WIDTH_A, WIDTH_B)], out_sem.at[1, c]),
        )

    tokens_copy = pltpu.make_async_copy(tok, tokens_out, load_sem.at[0])

    def partial_a(c):
        p = lax.rem(c, SLOTS)
        rows = pl.ds(c * CHUNK, CHUNK)
        act, grad = tok[0, rows, :], tok[1, rows, :]
        part_a[p, 0] = dot_nn(act, wg[:, :WIDTH_A])
        part_a[p, 1] = dot_nn(act, wu[:, :WIDTH_A])
        part_a[p, 2] = dot_nt(grad, wd[:WIDTH_A, :])
        for i in range(3):
            send_az[c, i] = part_a[p, i, pl.ds(64 * (1 - zl), 64), :].astype(BF16)
        send_az_copy(c).start()

    def partial_b(c):
        p = lax.rem(c, SLOTS)
        rows = pl.ds(c * CHUNK, CHUNK)
        act, grad = tok[0, rows, :], tok[1, rows, :]
        part_b[p, 0] = dot_nn(act, wg[:, WIDTH_A:])
        part_b[p, 1] = dot_nn(act, wu[:, WIDTH_A:])
        part_b[p, 2] = dot_nt(grad, wd[WIDTH_A:, :])
        for i in range(3):
            send_by[c, i] = part_b[p, i].astype(BF16)
        for k in range(4):
            by(c, k).start()

    def plane_a(c):
        p = lax.rem(c, SLOTS)
        send_az_copy(c).wait_recv()
        plane = pl.ds(64 * zl, 64)
        for i in range(3):
            total = part_a[p, i, plane, :] + recv_az[c, i].astype(F32)
            part_a[p, i, plane, :] = total
            send_ay[c, i] = total.astype(BF16)
        for k in range(4):
            ay(c, k).start()

    def ring_a(c):
        p = lax.rem(c, SLOTS)
        ay(c, 0).wait_recv()
        for i in range(3):
            total = part_a[p, i, pl.ds(64 * zl + OWN * y_next, OWN), :HALF_A] + recv_af[c, i].astype(F32)
            send_ay[c, i, pl.ds(OWN * y_next, OWN), :HALF_A] = total.astype(BF16)
        ay(c, 4).start()
        ay(c, 1).wait_recv()
        for i in range(3):
            total = part_a[p, i, pl.ds(64 * zl + OWN * y_prev, OWN), HALF_A:] + recv_as[c, i].astype(F32)
            send_ay[c, i, pl.ds(OWN * y_prev, OWN), HALF_A:] = total.astype(BF16)
        ay(c, 5).start()

    def ring_b(c):
        p = lax.rem(c, SLOTS)
        for side, y_ in ((0, y_next), (1, y_prev)):
            by(c, side).wait_recv()
            mine = pl.ds(32 * y_ + OWN * side, OWN)
            for i in range(3):
                total = part_b[p, i, mine, :] + recv_bu[c, side, i].astype(F32)
                send_by[c, i, mine, :] = total.astype(BF16)
            by(c, 4 + side).start()

    def own_a(c):
        p = lax.rem(c, SLOTS)
        for k in range(2, 6):
            ay(c, k).wait_recv()
        mine = pl.ds(64 * zl + OWN * y, OWN)
        sums = [
            part_a[p, i, mine, :] + recv_ay[c, 0, i].astype(F32) + recv_ay[c, 1, i].astype(F32)
            for i in range(3)
        ]
        for i, value in enumerate(swiglu_back(*sums)):
            delta_a[i, rows_a(c, y), :] = value
        for k in range(2):
            gather_ay(c, k, y).start()

    def own_b(c):
        p = lax.rem(c, SLOTS)
        for k in range(2, 6):
            by(c, k).wait_recv()
        for half in range(2):
            mine = pl.ds(32 * y + OWN * half, OWN)
            for i in range(3):
                total = part_b[p, i, mine, :]
                for side in range(2):
                    total = total + recv_by[c, side, i, pl.ds(OWN * half, OWN), :].astype(F32)
                part_b[p, i, mine, :] = total
        for i in range(3):
            send_bz[c, i] = part_b[p, i, pl.ds(32 * y + OWN * (1 - zl), OWN), :].astype(BF16)
        send_bz_copy(c).start()

    def point_b(c):
        p = lax.rem(c, SLOTS)
        send_bz_copy(c).wait_recv()
        mine = pl.ds(32 * y + OWN * zl, OWN)
        sums = [part_b[p, i, mine, :] + recv_bz[c, i].astype(F32) for i in range(3)]
        for i, value in enumerate(swiglu_back(*sums)):
            delta_b[i, rows_b(c, y, OWN * zl, OWN), :] = value
        gather_bz(c, zl).start()

    def forward_a(c):
        gather_ay(c, 0, y_prev).wait_recv()
        gather_ay(c, 2, y_prev).start()
        gather_ay(c, 1, y_next).wait_recv()
        gather_ay(c, 3, y_next).start()

    def quarter_b(c):
        gather_bz(c, 1 - zl).wait_recv()
        for k in range(2):
            gather_by(c, k, y).start()

    def swap_a(c):
        for k in (2, 3):
            gather_ay(c, k, y_far).wait_recv()
        gather_az(c, zl).start()

    def forward_b(c):
        gather_by(c, 0, y_prev).wait_recv()
        gather_by(c, 2, y_prev).start()
        gather_by(c, 1, y_next).wait_recv()
        gather_by(c, 3, y_next).start()

    def input_grad_part(c):
        rows = pl.ds(c * CHUNK, CHUNK)
        gather_az(c, 1 - zl).wait_recv()
        igrad[rows, :] = dot_nt(delta_a[1, rows, :], wg[:, :WIDTH_A])
        igrad[rows, :] += dot_nt(delta_a[2, rows, :], wu[:, :WIDTH_A])
        for k in (2, 3):
            gather_by(c, k, y_far).wait_recv()
        for copy in out_copies(c):
            copy.start()
        igrad[rows, :] += dot_nt(delta_b[1, rows, :], wg[:, WIDTH_A:])
        igrad[rows, :] += dot_nt(delta_b[2, rows, :], wu[:, WIDTH_A:])

    def unit_rows(unit, core_):
        return pl.ds(unit * UNIT + core_ * BLOCK, BLOCK)

    def core_copy(unit):
        return remote(
            igrad.at[unit_rows(unit, 1 - core)], core_recv.at[unit], core_s.at[unit], core_r.at[unit], sibling
        )

    def x_copy(unit):
        return remote(
            igrad.at[unit_rows(unit, core)], x_recv.at[unit - 1], x_s.at[unit - 1], x_r.at[unit - 1],
            at_x(unit_dist[unit]),
        )

    def sum_core(unit):
        core_copy(unit).wait_recv()
        rows = unit_rows(unit, core)
        igrad[rows, :] = igrad[rows, :] + core_recv[unit]
        if 1 <= unit <= 5:
            x_copy(unit).start()

    stages = (
        (6, input_grad_part), (5, swap_a), (5, forward_b), (4, forward_a), (4, quarter_b),
        (3, own_a), (3, point_b), (2, ring_a), (2, own_b), (1, plane_a), (1, ring_b),
        (0, partial_a), (0, partial_b),
    )
    units_done = ((0,), (1,), (2, 3), (4,), (5,), (6, 7))
    units_wait = ((), (2,), (3,), (4, 5), (6,), (7,))
    units_pass = ((2,), (7, 3), (4, 5), (6,), (), ())

    @pl.loop(0, CHUNKS + 6)
    def _(t):
        for delay, stage in stages:
            if delay == 0 and stage is partial_a:
                for c in range(1, CHUNKS):
                    @pl.when(t == c)
                    def _():
                        for unit in units_wait[c]:
                            to_sibling(unit).wait_recv()

            @pl.when((t >= delay) & (t < CHUNKS + delay))
            def _():
                stage(t - delay)

            if delay == 6:
                for c in range(CHUNKS):
                    @pl.when(t == c + 6)
                    def _():
                        for unit in units_done[c]:
                            core_copy(unit).start()

        for c in range(4):
            @pl.when(t == c)
            def _():
                for unit in units_pass[c]:
                    pass_on(unit)
                    if unit == 7:
                        for dist in (3, 1, 2):
                            to_x(1, dist).start()

        @pl.when(t == CHUNKS - 1)
        def _():
            tokens_copy.start()

        for c in range(CHUNKS - 1):
            @pl.when(t == c + 6)
            def _():
                for unit in units_done[c]:
                    sum_core(unit)

    near = igrad[unit_rows(0, core), :]
    for unit in (1, 2, 3):
        x_copy(unit).wait_recv()
        near = near + x_recv[unit - 1]
    near_out[...] = near
    for unit in (6, 7):
        sum_core(unit)
    far_out[...] = igrad[unit_rows(6, core), :]
    other = igrad[unit_rows(7, core), :]
    for unit in (4, 5):
        x_copy(unit).wait_recv()
        other = other + x_recv[unit - 1]
    other_out[...] = other

    to_zh().wait_send()
    for other_, dist in to_unit:
        to_x(other_, dist).wait_send()
    for unit in range(8):
        to_sibling(unit).wait_send()
        core_copy(unit).wait_send()
    for unit in range(1, 6):
        x_copy(unit).wait_send()

    @pl.loop(0, CHUNKS)
    def _(c):
        send_az_copy(c).wait_send()
        send_bz_copy(c).wait_send()
        gather_az(c, zl).wait_send()
        gather_bz(c, zl).wait_send()
        for k in range(6):
            ay(c, k).wait_send()
            by(c, k).wait_send()
        for k in range(4):
            gather_ay(c, k, y).wait_send()
            gather_by(c, k, y).wait_send()
        for copy in out_copies(c):
            copy.wait()

    tokens_copy.wait()


def exchange(activations, out_grad, w_gate, w_up, w_down):
    dma = pltpu.SemaphoreType.DMA
    any_spec = pl.BlockSpec(memory_space=pl.ANY)
    vmem_spec = pl.BlockSpec(memory_space=pltpu.VMEM)
    n = CHUNKS
    return pl.pallas_call(
        exchange_kernel,
        out_shape=[
            jax.ShapeDtypeStruct((2, TOKENS, D_LOCAL), BF16),
            jax.ShapeDtypeStruct((3, TOKENS, H_LOCAL), BF16),
            *[jax.ShapeDtypeStruct((BLOCK, D_LOCAL), F32)] * 3,
        ],
        in_specs=[any_spec] * 5,
        out_specs=[any_spec] * 2 + [vmem_spec] * 3,
        scratch_shapes=[
            pltpu.VMEM((D_LOCAL, H_LOCAL), BF16),
            pltpu.VMEM((D_LOCAL, H_LOCAL), BF16),
            pltpu.VMEM((H_LOCAL, D_LOCAL), BF16),
            pltpu.VMEM((2, TOKENS, D_LOCAL), BF16),
            pltpu.VMEM((SLOTS, 3, CHUNK, WIDTH_A), F32),
            pltpu.VMEM((SLOTS, 3, CHUNK, WIDTH_B), F32),
            pltpu.VMEM((n, 3, 64, WIDTH_A), BF16),
            pltpu.VMEM((n, 3, 64, WIDTH_A), BF16),
            pltpu.VMEM((n, 3, 64, WIDTH_A), BF16),
            pltpu.VMEM((n, 3, OWN, HALF_A), BF16),
            pltpu.VMEM((n, 3, OWN, WIDTH_A - HALF_A), BF16),
            pltpu.VMEM((n, 2, 3, OWN, WIDTH_A), BF16),
            pltpu.VMEM((n, 3, CHUNK, WIDTH_B), BF16),
            pltpu.VMEM((n, 2, 3, OWN, WIDTH_B), BF16),
            pltpu.VMEM((n, 2, 3, 32, WIDTH_B), BF16),
            pltpu.VMEM((n, 3, OWN, WIDTH_B), BF16),
            pltpu.VMEM((n, 3, OWN, WIDTH_B), BF16),
            pltpu.VMEM((3, TOKENS, WIDTH_A), BF16),
            pltpu.VMEM((3, TOKENS, WIDTH_B), BF16),
            pltpu.VMEM((TOKENS, D_LOCAL), F32),
            pltpu.VMEM((8, BLOCK, D_LOCAL), F32),
            pltpu.VMEM((5, BLOCK, D_LOCAL), F32),
            dma((5,)), dma((1,)), dma((1,)), dma((8,)), dma((8,)), dma((6,)), dma((6,)),
            *[dma((n,))] * 8,
            dma((n, 6)), dma((n, 6)), dma((n, 6)), dma((n, 6)),
            dma((n, 4)), dma((n, 4)), dma((n, 4)), dma((n, 4)),
            dma((8,)), dma((8,)), dma((5,)), dma((5,)),
            dma((2, n)),
        ],
        compiler_params=pltpu.CompilerParams(
            collective_id=0, has_side_effects=True, vmem_limit_bytes=60 * 2**20
        ),
        cost_estimate=pl.CostEstimate(
            flops=10 * TOKENS * D_LOCAL * H_LOCAL, bytes_accessed=22 * 2**20, transcendentals=0
        ),
        name="exchange",
    )(activations, out_grad, w_gate, w_up, w_down)


def weights_kernel(
    tok_in, delta_in, gate_out, up_out, down_out,
    tok, delta, gate, up, down, in_sem, out_sem,
):
    loads = [
        pltpu.make_async_copy(tok_in.at[0], tok.at[0], in_sem.at[0]),
        pltpu.make_async_copy(delta_in.at[1], delta.at[1], in_sem.at[1]),
        pltpu.make_async_copy(delta_in.at[2], delta.at[2], in_sem.at[2]),
        pltpu.make_async_copy(delta_in.at[0], delta.at[0], in_sem.at[3]),
        pltpu.make_async_copy(tok_in.at[1], tok.at[1], in_sem.at[4]),
    ]
    for load in loads:
        load.start()
    stores = []

    def store(src, dst, start, size):
        copy = pltpu.make_async_copy(
            src.at[pl.ds(start, size)], dst.at[pl.ds(start, size)], out_sem.at[len(stores)]
        )
        copy.start()
        stores.append(copy)

    loads[0].wait()
    for load, i, buf, out in ((loads[1], 1, gate, gate_out), (loads[2], 2, up, up_out)):
        load.wait()
        for m in range(0, D_LOCAL, 256):
            buf[m : m + 256, :] = dot_tn(tok[0, :, m : m + 256], delta[i]).astype(BF16)
            store(buf, out, m, 256)
    loads[3].wait()
    loads[4].wait()
    for m in range(0, H_LOCAL, 256):
        size = min(256, H_LOCAL - m)
        down[m : m + size, :] = dot_tn(delta[0, :, m : m + size], tok[1]).astype(BF16)
        store(down, down_out, m, size)
    for copy in stores:
        copy.wait()


def weight_grads(tokens, deltas):
    any_spec = pl.BlockSpec(memory_space=pl.ANY)
    shapes = [(D_LOCAL, H_LOCAL), (D_LOCAL, H_LOCAL), (H_LOCAL, D_LOCAL)]
    return pl.pallas_call(
        weights_kernel,
        out_shape=[jax.ShapeDtypeStruct(s, BF16) for s in shapes],
        in_specs=[any_spec] * 2,
        out_specs=[any_spec] * 3,
        scratch_shapes=[
            pltpu.VMEM((2, TOKENS, D_LOCAL), BF16),
            pltpu.VMEM((3, TOKENS, H_LOCAL), BF16),
            *[pltpu.VMEM(s, BF16) for s in shapes],
            pltpu.SemaphoreType.DMA((5,)),
            pltpu.SemaphoreType.DMA((15,)),
        ],
        compiler_params=pltpu.CompilerParams(vmem_limit_bytes=56 * 2**20),
        cost_estimate=pl.CostEstimate(
            flops=6 * TOKENS * D_LOCAL * H_LOCAL, bytes_accessed=22 * 2**20, transcendentals=0
        ),
        name="weight_grads",
    )(tokens, deltas)


def per_device(activations, out_grad, w_gate, w_up, w_down):
    tokens, deltas, near, other, far = exchange(activations, out_grad, w_gate, w_up, w_down)

    def moved(c, dist):
        return (1 - c // 8) * 8 + ((c // 2 + dist) % 4) * 2 + c % 2

    other = lax.ppermute(other, "col", [(c, moved(c, 0)) for c in range(16)])
    far = lax.ppermute(far, "col", [(c, moved(c, 2)) for c in range(16)])
    gate_grad, up_grad, down_grad = weight_grads(tokens, deltas)
    input_grad = (near + other + far).astype(BF16)
    return input_grad, gate_grad, up_grad, down_grad


def solution(mesh):
    placed = (P("col", "row"), P("col", "row"), P("row", "col"), P("row", "col"), P("col", "row"))
    return jax.shard_map(
        per_device,
        mesh=mesh,
        in_specs=placed,
        out_specs=(P("col", "row"), P("row", "col"), P("row", "col"), P("col", "row")),
        check_vma=False,
    )
```

```python
import functools

import jax
import jax.numpy as jnp
from jax import lax
from jax.experimental import pallas as pl
from jax.experimental.pallas import tpu as pltpu
from jax.sharding import PartitionSpec as P

F32 = jnp.float32
BF16 = jnp.bfloat16
MESH = pl.DeviceIdType.MESH

CHUNKS = 6
CHUNK = 128
OWN = 16
SLOTS = 4
D_LOCAL = 1024
H_LOCAL = 1664
TOKENS = 768
BLOCK = 48
WIDTH_A = 768
HALF_A = 384
WIDTH_B = H_LOCAL - WIDTH_A
LEAD = 32
BLOCK_ORDER = (
    (0, 0), (0, 1), (1, 0), (2, 0), (3, 0), (1, 1), (2, 1), (3, 1),
    (4, 0), (4, 1), (5, 0), (5, 1), (6, 0), (6, 1), (7, 0), (7, 1),
)


def dot_nn(a, b):
    return jnp.dot(a, b, preferred_element_type=F32)


def dot_nt(a, b):
    return lax.dot_general(a, b, (((1,), (1,)), ((), ())), preferred_element_type=F32)


def dot_tn(a, b):
    return lax.dot_general(a, b, (((0,), (0,)), ((), ())), preferred_element_type=F32)


def swiglu_back(gate, upper, hidden_grad):
    sig = jax.nn.sigmoid(gate)
    act = gate * sig
    hidden = (act * upper).astype(BF16)
    gate_delta = (hidden_grad * upper * sig * (1.0 + gate * (1.0 - sig))).astype(BF16)
    up_delta = (hidden_grad * act).astype(BF16)
    return hidden, gate_delta, up_delta


def exchange_kernel(
    act_in, grad_in, wg_in, wu_in, wd_in,
    tokens_out, delta_out, near_out, other_out,
    wg, wu, wd, tok, part_a, part_b,
    send_az, recv_az, send_ay, recv_af, recv_as, recv_ay,
    send_by, recv_bu, recv_by, send_bz, recv_bz,
    delta_a, delta_b, igrad, core_recv, x_recv,
    load_sem, zh_s, zh_r, sib_s, sib_r, tokx_s, tokx_r,
    az_s, az_r, bz_s, bz_r, gaz_s, gaz_r, gbz_s, gbz_r,
    ay_s, ay_r, by_s, by_r, gay_s, gay_r, gby_s, gby_r,
    core_s, core_r, x_s, x_r, out_sem,
):
    row = lax.axis_index("row")
    col = lax.axis_index("col")
    y = lax.rem(row, 4)
    zl = lax.div(row, 4)
    zh = lax.div(col, 8)
    x = lax.rem(lax.div(col, 2), 4)
    core = lax.rem(col, 2)
    y_next, y_prev, y_far = lax.rem(y + 1, 4), lax.rem(y + 3, 4), lax.rem(y + 2, 4)

    def at_x(dist):
        return (row, zh * 8 + lax.rem(x + dist, 4) * 2 + core)

    up_y = (zl * 4 + y_next, col)
    down_y = (zl * 4 + y_prev, col)
    z_pair = ((1 - zl) * 4 + y, col)
    zh_pair = (row, (1 - zh) * 8 + x * 2 + core)
    sibling = (row, zh * 8 + x * 2 + 1 - core)
    partners = [up_y, down_y, z_pair, at_x(1), at_x(2), at_x(3), zh_pair, sibling]

    def remote(src, dst, send, recv, device):
        return pltpu.make_async_remote_copy(
            src_ref=src, dst_ref=dst, send_sem=send, recv_sem=recv,
            device_id=device, device_id_type=MESH,
        )

    unit_dist = (0, 1, 3, 2, 2, 1, 3, 0)
    to_unit = {(0, 3): 1, (0, 1): 2, (0, 2): 3, (1, 2): 4, (1, 3): 5, (1, 1): 6}

    def at(unit, other_core):
        return BLOCK * BLOCK_ORDER.index((unit, other_core))

    def blk(unit, other_core):
        return tok.at[:, pl.ds(at(unit, other_core), BLOCK)]

    def to_zh():
        return remote(blk(0, 0), blk(7, 0), zh_s.at[0], zh_r.at[0], zh_pair)

    def to_sibling(unit):
        return remote(blk(unit, 0), blk(unit, 1), sib_s.at[unit], sib_r.at[unit], sibling)

    def to_x(other, dist):
        unit = to_unit[other, dist]
        return remote(blk(7 * other, 0), blk(unit, 0), tokx_s.at[unit - 1], tokx_r.at[unit - 1], at_x(dist))

    def pass_on(unit):
        if unit == 7:
            to_zh().wait_recv()
            for dist in (2, 3, 1):
                to_x(1, dist).start()
        else:
            view = blk(unit, 0)
            remote(view, view, tokx_s.at[unit - 1], tokx_r.at[unit - 1], at_x(unit_dist[unit])).wait_recv()
        to_sibling(unit).start()

    again = pl.ds(TOKENS, LEAD)
    loads = [
        pltpu.make_async_copy(act_in, tok.at[0, pl.ds(0, BLOCK)], load_sem.at[0]),
        pltpu.make_async_copy(grad_in, tok.at[1, pl.ds(0, BLOCK)], load_sem.at[1]),
        pltpu.make_async_copy(act_in.at[pl.ds(0, LEAD)], tok.at[0, again], load_sem.at[2]),
        pltpu.make_async_copy(grad_in.at[pl.ds(0, LEAD)], tok.at[1, again], load_sem.at[3]),
        pltpu.make_async_copy(wg_in, wg, load_sem.at[4]),
        pltpu.make_async_copy(wu_in, wu, load_sem.at[5]),
        pltpu.make_async_copy(wd_in, wd, load_sem.at[6]),
    ]
    for load in loads:
        load.start()

    barrier = pltpu.get_barrier_semaphore()
    for device in partners:
        pl.semaphore_signal(barrier, inc=1, device_id=device, device_id_type=MESH)
    pl.semaphore_wait(barrier, len(partners))

    loads[0].wait()
    loads[1].wait()
    to_x(0, 3).start()
    to_x(0, 1).start()
    to_sibling(0).start()
    to_zh().start()
    to_x(0, 2).start()
    for load in loads[2:]:
        load.wait()
    to_sibling(0).wait_recv()
    pass_on(1)
    pass_on(2)

    def rows_a(c, y_):
        return pl.ds(c * CHUNK + 64 * zl + OWN * y_, OWN)

    def rows_b(c, y_, first, size):
        return pl.ds(c * CHUNK + 32 * y_ + first, size)

    first_a, second_a = pl.ds(0, HALF_A), pl.ds(HALF_A, WIDTH_A - HALF_A)

    def send_az_copy(c):
        return remote(send_az.at[c], recv_az.at[c], az_s.at[c], az_r.at[c], z_pair)

    def send_bz_copy(c):
        return remote(send_bz.at[c], recv_bz.at[c], bz_s.at[c], bz_r.at[c], z_pair)

    def ay(c, k):
        def src(y_, cols):
            return send_ay.at[c, :, pl.ds(OWN * y_, OWN), cols]

        sem = (ay_s.at[c, k], ay_r.at[c, k])
        if k == 0:
            return remote(src(y_far, first_a), recv_af.at[c], *sem, up_y)
        if k == 1:
            return remote(src(y_far, second_a), recv_as.at[c], *sem, down_y)
        if k == 2:
            return remote(src(y_next, second_a), recv_ay.at[c, 0, :, :, second_a], *sem, up_y)
        if k == 3:
            return remote(src(y_prev, first_a), recv_ay.at[c, 1, :, :, first_a], *sem, down_y)
        if k == 4:
            return remote(src(y_next, first_a), recv_ay.at[c, 0, :, :, first_a], *sem, up_y)
        return remote(src(y_prev, second_a), recv_ay.at[c, 1, :, :, second_a], *sem, down_y)

    def by(c, k):
        def src(y_, half):
            return send_by.at[c, :, pl.ds(32 * y_ + OWN * half, OWN)]

        def dst(side, half):
            return recv_by.at[c, side, :, pl.ds(OWN * half, OWN)]

        sem = (by_s.at[c, k], by_r.at[c, k])
        if k == 0:
            return remote(src(y_far, 0), recv_bu.at[c, 0], *sem, up_y)
        if k == 1:
            return remote(src(y_far, 1), recv_bu.at[c, 1], *sem, down_y)
        if k == 2:
            return remote(src(y_next, 1), dst(0, 1), *sem, up_y)
        if k == 3:
            return remote(src(y_prev, 0), dst(1, 0), *sem, down_y)
        if k == 4:
            return remote(src(y_next, 0), dst(0, 0), *sem, up_y)
        return remote(src(y_prev, 1), dst(1, 1), *sem, down_y)

    def same(view, send, recv, device):
        return remote(view, view, send, recv, device)

    def gather_az(c, zl_):
        view = delta_a.at[:, pl.ds(c * CHUNK + 64 * zl_, 64)]
        return same(view, gaz_s.at[c], gaz_r.at[c], z_pair)

    def gather_bz(c, zl_):
        return same(delta_b.at[:, rows_b(c, y, OWN * zl_, OWN)], gbz_s.at[c], gbz_r.at[c], z_pair)

    def gather_ay(c, k, y_):
        sem = (gay_s.at[c, k], gay_r.at[c, k])
        rows = rows_a(c, y_)
        view = (delta_a.at[:, rows], delta_a.at[:, rows],
                delta_a.at[:, rows, second_a], delta_a.at[:, rows, first_a])[k]
        return same(view, *sem, down_y if k % 2 else up_y)

    def gather_by(c, k, y_):
        sem = (gby_s.at[c, k], gby_r.at[c, k])
        rows = (rows_b(c, y_, 0, 32), rows_b(c, y_, 0, 32), rows_b(c, y_, OWN, OWN), rows_b(c, y_, 0, OWN))[k]
        return same(delta_b.at[:, rows], *sem, down_y if k % 2 else up_y)

    def out_copies(c):
        rows = pl.ds(c * CHUNK, CHUNK)
        return (
            pltpu.make_async_copy(delta_a.at[:, rows], delta_out.at[:, rows, pl.ds(0, WIDTH_A)], out_sem.at[0, c]),
            pltpu.make_async_copy(delta_b.at[:, rows], delta_out.at[:, rows, pl.ds(WIDTH_A, WIDTH_B)], out_sem.at[1, c]),
        )

    tokens_copy = pltpu.make_async_copy(tok.at[:, pl.ds(LEAD, TOKENS)], tokens_out, load_sem.at[0])

    def partial_a(c):
        p = lax.rem(c, SLOTS)
        rows = pl.ds(LEAD + c * CHUNK, CHUNK)
        act, grad = tok[0, rows, :], tok[1, rows, :]
        part_a[p, 0] = dot_nn(act, wg[:, :WIDTH_A])
        part_a[p, 1] = dot_nn(act, wu[:, :WIDTH_A])
        part_a[p, 2] = dot_nt(grad, wd[:WIDTH_A, :])
        for i in range(3):
            send_az[c, i] = part_a[p, i, pl.ds(64 * (1 - zl), 64), :].astype(BF16)
        send_az_copy(c).start()

    def partial_b(c):
        p = lax.rem(c, SLOTS)
        rows = pl.ds(LEAD + c * CHUNK, CHUNK)
        act, grad = tok[0, rows, :], tok[1, rows, :]
        part_b[p, 0] = dot_nn(act, wg[:, WIDTH_A:])
        part_b[p, 1] = dot_nn(act, wu[:, WIDTH_A:])
        part_b[p, 2] = dot_nt(grad, wd[WIDTH_A:, :])
        for i in range(3):
            send_by[c, i] = part_b[p, i].astype(BF16)
        for k in range(4):
            by(c, k).start()

    def plane_a(c):
        p = lax.rem(c, SLOTS)
        send_az_copy(c).wait_recv()
        plane = pl.ds(64 * zl, 64)
        for i in range(3):
            total = part_a[p, i, plane, :] + recv_az[c, i].astype(F32)
            part_a[p, i, plane, :] = total
            send_ay[c, i] = total.astype(BF16)
        for k in range(4):
            ay(c, k).start()

    def ring_a(c):
        p = lax.rem(c, SLOTS)
        ay(c, 0).wait_recv()
        for i in range(3):
            total = part_a[p, i, pl.ds(64 * zl + OWN * y_next, OWN), :HALF_A] + recv_af[c, i].astype(F32)
            send_ay[c, i, pl.ds(OWN * y_next, OWN), :HALF_A] = total.astype(BF16)
        ay(c, 4).start()
        ay(c, 1).wait_recv()
        for i in range(3):
            total = part_a[p, i, pl.ds(64 * zl + OWN * y_prev, OWN), HALF_A:] + recv_as[c, i].astype(F32)
            send_ay[c, i, pl.ds(OWN * y_prev, OWN), HALF_A:] = total.astype(BF16)
        ay(c, 5).start()

    def ring_b(c):
        p = lax.rem(c, SLOTS)
        for side, y_ in ((0, y_next), (1, y_prev)):
            by(c, side).wait_recv()
            mine = pl.ds(32 * y_ + OWN * side, OWN)
            for i in range(3):
                total = part_b[p, i, mine, :] + recv_bu[c, side, i].astype(F32)
                send_by[c, i, mine, :] = total.astype(BF16)
            by(c, 4 + side).start()

    def own_a(c):
        p = lax.rem(c, SLOTS)
        for k in range(2, 6):
            ay(c, k).wait_recv()
        mine = pl.ds(64 * zl + OWN * y, OWN)
        sums = [
            part_a[p, i, mine, :] + recv_ay[c, 0, i].astype(F32) + recv_ay[c, 1, i].astype(F32)
            for i in range(3)
        ]
        for i, value in enumerate(swiglu_back(*sums)):
            delta_a[i, rows_a(c, y), :] = value
        for k in range(2):
            gather_ay(c, k, y).start()

    def own_b(c):
        p = lax.rem(c, SLOTS)
        for k in range(2, 6):
            by(c, k).wait_recv()
        for half in range(2):
            mine = pl.ds(32 * y + OWN * half, OWN)
            for i in range(3):
                total = part_b[p, i, mine, :]
                for side in range(2):
                    total = total + recv_by[c, side, i, pl.ds(OWN * half, OWN), :].astype(F32)
                part_b[p, i, mine, :] = total
        for i in range(3):
            send_bz[c, i] = part_b[p, i, pl.ds(32 * y + OWN * (1 - zl), OWN), :].astype(BF16)
        send_bz_copy(c).start()

    def point_b(c):
        p = lax.rem(c, SLOTS)
        send_bz_copy(c).wait_recv()
        mine = pl.ds(32 * y + OWN * zl, OWN)
        sums = [part_b[p, i, mine, :] + recv_bz[c, i].astype(F32) for i in range(3)]
        for i, value in enumerate(swiglu_back(*sums)):
            delta_b[i, rows_b(c, y, OWN * zl, OWN), :] = value
        gather_bz(c, zl).start()

    def forward_a(c):
        gather_ay(c, 0, y_prev).wait_recv()
        gather_ay(c, 2, y_prev).start()
        gather_ay(c, 1, y_next).wait_recv()
        gather_ay(c, 3, y_next).start()

    def quarter_b(c):
        gather_bz(c, 1 - zl).wait_recv()
        for k in range(2):
            gather_by(c, k, y).start()

    def swap_a(c):
        for k in (2, 3):
            gather_ay(c, k, y_far).wait_recv()
        gather_az(c, zl).start()

    def forward_b(c):
        gather_by(c, 0, y_prev).wait_recv()
        gather_by(c, 2, y_prev).start()
        gather_by(c, 1, y_next).wait_recv()
        gather_by(c, 3, y_next).start()

    def input_grad_a(c):
        rows, out = pl.ds(c * CHUNK, CHUNK), pl.ds(LEAD + c * CHUNK, CHUNK)
        gather_az(c, 1 - zl).wait_recv()
        igrad[out, :] = dot_nt(delta_a[1, rows, :], wg[:, :WIDTH_A])
        igrad[out, :] += dot_nt(delta_a[2, rows, :], wu[:, :WIDTH_A])

    def input_grad_b(c):
        rows, out = pl.ds(c * CHUNK, CHUNK), pl.ds(LEAD + c * CHUNK, CHUNK)
        for k in (2, 3):
            gather_by(c, k, y_far).wait_recv()
        for copy in out_copies(c):
            copy.start()
        igrad[out, :] += dot_nt(delta_b[1, rows, :], wg[:, WIDTH_A:])
        igrad[out, :] += dot_nt(delta_b[2, rows, :], wu[:, WIDTH_A:])

    def core_copy(unit):
        src = igrad.at[pl.ds(at(unit, 1), BLOCK)]
        return remote(src, core_recv.at[unit], core_s.at[unit], core_r.at[unit], sibling)

    def x_copy(unit):
        src = igrad.at[pl.ds(at(unit, 0), BLOCK)]
        return remote(src, x_recv.at[unit - 1], x_s.at[unit - 1], x_r.at[unit - 1], at_x(unit_dist[unit]))

    def sum_core(unit):
        core_copy(unit).wait_recv()
        rows = pl.ds(at(unit, 0), BLOCK)
        igrad[rows, :] = igrad[rows, :] + core_recv[unit]
        x_copy(unit).start()

    stages = (
        (0, partial_a), (5, swap_a), (0, partial_b), (4, forward_a), (1, ring_b), (1, plane_a), (2, own_b),
        (3, point_b), (3, own_a), (2, ring_a), (4, quarter_b), (5, forward_b), (6, input_grad_a), (6, input_grad_b),
    )
    units_done = ((0,), (1,), (2, 3), (4,), (5, 6), (7,))
    units_wait = ((), (1,), (2, 3), (4, 5), (6,), (7,))
    units_pass = ((3, 7), (4, 5), (6,))

    first = [stage for delay, stage in stages if delay == 0][0]
    last = max(delay for delay, _ in stages)

    @pl.loop(0, CHUNKS + last)
    def _(t):
        for delay, stage in stages:
            if stage is first:
                for c in range(1, CHUNKS):
                    @pl.when(t == c)
                    def _():
                        for unit in units_wait[c]:
                            to_sibling(unit).wait_recv()

            @pl.when((t >= delay) & (t < CHUNKS + delay))
            def _():
                stage(t - delay)

            if stage is input_grad_b:
                for c in range(CHUNKS):
                    @pl.when(t == c + last)
                    def _():
                        for unit in units_done[c]:
                            core_copy(unit).start()

        for c, units in enumerate(units_pass):
            @pl.when(t == c)
            def _():
                for unit in units:
                    pass_on(unit)

        @pl.when(t == CHUNKS - 1)
        def _():
            tokens_copy.start()

        for c in range(CHUNKS - 1):
            @pl.when(t == c + last)
            def _():
                for unit in units_done[c]:
                    if unit:
                        sum_core(unit)

    core_copy(0).wait_recv()
    near = igrad[pl.ds(at(0, 0) + LEAD, BLOCK - LEAD), :], igrad[again, :]
    near = jnp.concatenate([near[1], near[0]], axis=0) + core_recv[0]
    for unit in (1, 2, 3):
        x_copy(unit).wait_recv()
        near = near + x_recv[unit - 1]
    near_out[...] = near
    core_copy(7).wait_recv()
    other = igrad[pl.ds(at(7, 0), BLOCK), :] + core_recv[7]
    for unit in (4, 5, 6):
        x_copy(unit).wait_recv()
        other = other + x_recv[unit - 1]
    other_out[...] = other

    to_zh().wait_send()
    for other_, dist in to_unit:
        to_x(other_, dist).wait_send()
    for unit in range(8):
        to_sibling(unit).wait_send()
        core_copy(unit).wait_send()
    for unit in range(1, 7):
        x_copy(unit).wait_send()

    @pl.loop(0, CHUNKS)
    def _(c):
        send_az_copy(c).wait_send()
        send_bz_copy(c).wait_send()
        gather_az(c, zl).wait_send()
        gather_bz(c, zl).wait_send()
        for k in range(6):
            ay(c, k).wait_send()
            by(c, k).wait_send()
        for k in range(4):
            gather_ay(c, k, y).wait_send()
            gather_by(c, k, y).wait_send()
        for copy in out_copies(c):
            copy.wait()

    tokens_copy.wait()


def exchange(activations, out_grad, w_gate, w_up, w_down):
    dma = pltpu.SemaphoreType.DMA
    any_spec = pl.BlockSpec(memory_space=pl.ANY)
    vmem_spec = pl.BlockSpec(memory_space=pltpu.VMEM)
    n = CHUNKS
    return pl.pallas_call(
        exchange_kernel,
        out_shape=[
            jax.ShapeDtypeStruct((2, TOKENS, D_LOCAL), BF16),
            jax.ShapeDtypeStruct((3, TOKENS, H_LOCAL), BF16),
            *[jax.ShapeDtypeStruct((BLOCK, D_LOCAL), F32)] * 2,
        ],
        in_specs=[any_spec] * 5,
        out_specs=[any_spec] * 2 + [vmem_spec] * 2,
        scratch_shapes=[
            pltpu.VMEM((D_LOCAL, H_LOCAL), BF16),
            pltpu.VMEM((D_LOCAL, H_LOCAL), BF16),
            pltpu.VMEM((H_LOCAL, D_LOCAL), BF16),
            pltpu.VMEM((2, TOKENS + LEAD, D_LOCAL), BF16),
            pltpu.VMEM((SLOTS, 3, CHUNK, WIDTH_A), F32),
            pltpu.VMEM((SLOTS, 3, CHUNK, WIDTH_B), F32),
            pltpu.VMEM((n, 3, 64, WIDTH_A), BF16),
            pltpu.VMEM((n, 3, 64, WIDTH_A), BF16),
            pltpu.VMEM((n, 3, 64, WIDTH_A), BF16),
            pltpu.VMEM((n, 3, OWN, HALF_A), BF16),
            pltpu.VMEM((n, 3, OWN, WIDTH_A - HALF_A), BF16),
            pltpu.VMEM((n, 2, 3, OWN, WIDTH_A), BF16),
            pltpu.VMEM((n, 3, CHUNK, WIDTH_B), BF16),
            pltpu.VMEM((n, 2, 3, OWN, WIDTH_B), BF16),
            pltpu.VMEM((n, 2, 3, 32, WIDTH_B), BF16),
            pltpu.VMEM((n, 3, OWN, WIDTH_B), BF16),
            pltpu.VMEM((n, 3, OWN, WIDTH_B), BF16),
            pltpu.VMEM((3, TOKENS, WIDTH_A), BF16),
            pltpu.VMEM((3, TOKENS, WIDTH_B), BF16),
            pltpu.VMEM((TOKENS + LEAD, D_LOCAL), F32),
            pltpu.VMEM((8, BLOCK, D_LOCAL), F32),
            pltpu.VMEM((6, BLOCK, D_LOCAL), F32),
            dma((7,)), dma((1,)), dma((1,)), dma((8,)), dma((8,)), dma((6,)), dma((6,)),
            *[dma((n,))] * 8,
            dma((n, 6)), dma((n, 6)), dma((n, 6)), dma((n, 6)),
            dma((n, 4)), dma((n, 4)), dma((n, 4)), dma((n, 4)),
            dma((8,)), dma((8,)), dma((6,)), dma((6,)),
            dma((2, n)),
        ],
        compiler_params=pltpu.CompilerParams(
            collective_id=0, has_side_effects=True, vmem_limit_bytes=60 * 2**20
        ),
        cost_estimate=pl.CostEstimate(
            flops=10 * TOKENS * D_LOCAL * H_LOCAL, bytes_accessed=22 * 2**20, transcendentals=0
        ),
        name="exchange",
    )(activations, out_grad, w_gate, w_up, w_down)


def weights_kernel(
    tok_in, delta_in, gate_out, up_out, down_out,
    tok, delta, gate, up, down, in_sem, out_sem,
):
    loads = [
        pltpu.make_async_copy(tok_in.at[0], tok.at[0], in_sem.at[0]),
        pltpu.make_async_copy(delta_in.at[1], delta.at[1], in_sem.at[1]),
        pltpu.make_async_copy(delta_in.at[2], delta.at[2], in_sem.at[2]),
        pltpu.make_async_copy(delta_in.at[0], delta.at[0], in_sem.at[3]),
        pltpu.make_async_copy(tok_in.at[1], tok.at[1], in_sem.at[4]),
    ]
    for load in loads:
        load.start()
    stores = []

    def store(src, dst, start, size):
        copy = pltpu.make_async_copy(
            src.at[pl.ds(start, size)], dst.at[pl.ds(start, size)], out_sem.at[len(stores)]
        )
        copy.start()
        stores.append(copy)

    loads[0].wait()
    for load, i, buf, out in ((loads[1], 1, gate, gate_out), (loads[2], 2, up, up_out)):
        load.wait()
        for m in range(0, D_LOCAL, 256):
            buf[m : m + 256, :] = dot_tn(tok[0, :, m : m + 256], delta[i]).astype(BF16)
            store(buf, out, m, 256)
    loads[3].wait()
    loads[4].wait()
    for m in range(0, H_LOCAL, 256):
        size = min(256, H_LOCAL - m)
        down[m : m + size, :] = dot_tn(delta[0, :, m : m + size], tok[1]).astype(BF16)
        store(down, down_out, m, size)
    for copy in stores:
        copy.wait()


def weight_grads(tokens, deltas):
    any_spec = pl.BlockSpec(memory_space=pl.ANY)
    shapes = [(D_LOCAL, H_LOCAL), (D_LOCAL, H_LOCAL), (H_LOCAL, D_LOCAL)]
    return pl.pallas_call(
        weights_kernel,
        out_shape=[jax.ShapeDtypeStruct(s, BF16) for s in shapes],
        in_specs=[any_spec] * 2,
        out_specs=[any_spec] * 3,
        scratch_shapes=[
            pltpu.VMEM((2, TOKENS, D_LOCAL), BF16),
            pltpu.VMEM((3, TOKENS, H_LOCAL), BF16),
            *[pltpu.VMEM(s, BF16) for s in shapes],
            pltpu.SemaphoreType.DMA((5,)),
            pltpu.SemaphoreType.DMA((15,)),
        ],
        compiler_params=pltpu.CompilerParams(vmem_limit_bytes=56 * 2**20),
        cost_estimate=pl.CostEstimate(
            flops=6 * TOKENS * D_LOCAL * H_LOCAL, bytes_accessed=22 * 2**20, transcendentals=0
        ),
        name="weight_grads",
    )(tokens, deltas)


def per_device(activations, out_grad, w_gate, w_up, w_down):
    tokens, deltas, near, other = exchange(activations, out_grad, w_gate, w_up, w_down)
    other = lax.ppermute(other, "col", [(c, (c + 8) % 16) for c in range(16)])
    gate_grad, up_grad, down_grad = weight_grads(tokens, deltas)
    return (near + other).astype(BF16), gate_grad, up_grad, down_grad


def solution(mesh):
    placed = (P("col", "row"), P("col", "row"), P("row", "col"), P("row", "col"), P("col", "row"))
    return jax.shard_map(
        per_device,
        mesh=mesh,
        in_specs=placed,
        out_specs=(P("col", "row"), P("row", "col"), P("row", "col"), P("col", "row")),
        check_vma=False,
    )
```

```python
import functools

import jax
import jax.numpy as jnp
from jax import lax
from jax.experimental import pallas as pl
from jax.experimental.pallas import tpu as pltpu
from jax.sharding import PartitionSpec as P

F32 = jnp.float32
BF16 = jnp.bfloat16
MESH = pl.DeviceIdType.MESH

CHUNKS = 6
CHUNK = 128
OWN = 16
SLOTS = 4
D_LOCAL = 1024
H_LOCAL = 1664
TOKENS = 768
BLOCK = 48
WIDTH_A = 768
HALF_A = 384
WIDTH_B = H_LOCAL - WIDTH_A
LEAD = 32
BLOCK_ORDER = (
    (0, 0), (0, 1), (1, 0), (2, 0), (3, 0), (1, 1), (2, 1), (3, 1),
    (4, 0), (4, 1), (5, 0), (5, 1), (6, 0), (6, 1), (7, 0), (7, 1),
)


def dot_nn(a, b):
    return jnp.dot(a, b, preferred_element_type=F32)


def dot_nt(a, b):
    return lax.dot_general(a, b, (((1,), (1,)), ((), ())), preferred_element_type=F32)


def dot_tn(a, b):
    return lax.dot_general(a, b, (((0,), (0,)), ((), ())), preferred_element_type=F32)


def swiglu_back(gate, upper, hidden_grad):
    sig = jax.nn.sigmoid(gate)
    act = gate * sig
    hidden = (act * upper).astype(BF16)
    gate_delta = (hidden_grad * upper * sig * (1.0 + gate * (1.0 - sig))).astype(BF16)
    up_delta = (hidden_grad * act).astype(BF16)
    return hidden, gate_delta, up_delta


def exchange_kernel(
    act_in, grad_in, wg_in, wu_in, wd_in,
    tokens_out, delta_out, near_out, other_out,
    wg, wu, wd, tok, part_a, part_b,
    send_az, recv_az, send_ay, recv_af, recv_as, recv_ay,
    send_by, recv_bu, recv_by, send_bz, recv_bz,
    delta_a, delta_b, igrad, core_recv, x_recv,
    load_sem, zh_s, zh_r, sib_s, sib_r, tokx_s, tokx_r,
    az_s, az_r, bz_s, bz_r, gaz_s, gaz_r, gbz_s, gbz_r,
    ay_s, ay_r, by_s, by_r, gay_s, gay_r, gby_s, gby_r,
    core_s, core_r, x_s, x_r, out_sem,
):
    row = lax.axis_index("row")
    col = lax.axis_index("col")
    y = lax.rem(row, 4)
    zl = lax.div(row, 4)
    zh = lax.div(col, 8)
    x = lax.rem(lax.div(col, 2), 4)
    core = lax.rem(col, 2)
    y_next, y_prev, y_far = lax.rem(y + 1, 4), lax.rem(y + 3, 4), lax.rem(y + 2, 4)

    def at_x(dist):
        return (row, zh * 8 + lax.rem(x + dist, 4) * 2 + core)

    up_y = (zl * 4 + y_next, col)
    down_y = (zl * 4 + y_prev, col)
    z_pair = ((1 - zl) * 4 + y, col)
    zh_pair = (row, (1 - zh) * 8 + x * 2 + core)
    sibling = (row, zh * 8 + x * 2 + 1 - core)
    partners = [up_y, down_y, z_pair, at_x(1), at_x(2), at_x(3), zh_pair, sibling]

    def remote(src, dst, send, recv, device):
        return pltpu.make_async_remote_copy(
            src_ref=src, dst_ref=dst, send_sem=send, recv_sem=recv,
            device_id=device, device_id_type=MESH,
        )

    unit_dist = (0, 1, 3, 2, 2, 1, 3, 0)
    to_unit = {(0, 3): 1, (0, 1): 2, (0, 2): 3, (1, 2): 4, (1, 3): 5, (1, 1): 6}

    def at(unit, other_core):
        return BLOCK * BLOCK_ORDER.index((unit, other_core))

    def blk(i, unit, other_core):
        return tok.at[i, pl.ds(at(unit, other_core), BLOCK)]

    def to_zh(i):
        return remote(blk(i, 0, 0), blk(i, 7, 0), zh_s.at[i], zh_r.at[i], zh_pair)

    def to_sibling(i, unit):
        return remote(blk(i, unit, 0), blk(i, unit, 1), sib_s.at[i, unit], sib_r.at[i, unit], sibling)

    def to_x(i, other, dist):
        unit = to_unit[other, dist]
        return remote(blk(i, 7 * other, 0), blk(i, unit, 0), tokx_s.at[i, unit - 1], tokx_r.at[i, unit - 1], at_x(dist))

    def pass_on(i, unit):
        if unit == 7:
            to_zh(i).wait_recv()
            for dist in (2, 3, 1):
                to_x(i, 1, dist).start()
        else:
            view = blk(i, unit, 0)
            remote(view, view, tokx_s.at[i, unit - 1], tokx_r.at[i, unit - 1], at_x(unit_dist[unit])).wait_recv()
        to_sibling(i, unit).start()

    again = pl.ds(TOKENS, LEAD)
    loads = [
        pltpu.make_async_copy(act_in, tok.at[0, pl.ds(0, BLOCK)], load_sem.at[0]),
        pltpu.make_async_copy(grad_in, tok.at[1, pl.ds(0, BLOCK)], load_sem.at[1]),
        pltpu.make_async_copy(act_in.at[pl.ds(0, LEAD)], tok.at[0, again], load_sem.at[2]),
        pltpu.make_async_copy(grad_in.at[pl.ds(0, LEAD)], tok.at[1, again], load_sem.at[3]),
        pltpu.make_async_copy(wg_in, wg, load_sem.at[4]),
        pltpu.make_async_copy(wu_in, wu, load_sem.at[5]),
        pltpu.make_async_copy(wd_in, wd, load_sem.at[6]),
    ]
    barrier = pltpu.get_barrier_semaphore()
    for device in partners:
        pl.semaphore_signal(barrier, inc=1, device_id=device, device_id_type=MESH)
    for load in loads:
        load.start()
    pl.semaphore_wait(barrier, len(partners))

    loads[0].wait()
    loads[1].wait()
    for i in range(2):
        to_x(i, 0, 3).start()
        to_x(i, 0, 1).start()
        to_sibling(i, 0).start()
    for i in range(2):
        to_zh(i).start()
        to_x(i, 0, 2).start()

    def first_tokens(i):
        to_sibling(i, 0).wait_recv()
        pass_on(i, 1)
        pass_on(i, 2)

    for load in loads[2:6]:
        load.wait()
    first_tokens(0)

    def rows_a(c, y_):
        return pl.ds(c * CHUNK + 64 * zl + OWN * y_, OWN)

    def rows_b(c, y_, first, size):
        return pl.ds(c * CHUNK + 32 * y_ + first, size)

    first_a, second_a = pl.ds(0, HALF_A), pl.ds(HALF_A, WIDTH_A - HALF_A)

    def send_az_copy(c, i):
        return remote(send_az.at[c, i], recv_az.at[c, i], az_s.at[c, i], az_r.at[c, i], z_pair)

    def send_bz_copy(c):
        return remote(send_bz.at[c], recv_bz.at[c], bz_s.at[c], bz_r.at[c], z_pair)

    def ay(c, k):
        def src(y_, cols):
            return send_ay.at[c, :, pl.ds(OWN * y_, OWN), cols]

        sem = (ay_s.at[c, k], ay_r.at[c, k])
        if k == 0:
            return remote(src(y_far, first_a), recv_af.at[c], *sem, up_y)
        if k == 1:
            return remote(src(y_far, second_a), recv_as.at[c], *sem, down_y)
        if k == 2:
            return remote(src(y_next, second_a), recv_ay.at[c, 0, :, :, second_a], *sem, up_y)
        if k == 3:
            return remote(src(y_prev, first_a), recv_ay.at[c, 1, :, :, first_a], *sem, down_y)
        if k == 4:
            return remote(src(y_next, first_a), recv_ay.at[c, 0, :, :, first_a], *sem, up_y)
        return remote(src(y_prev, second_a), recv_ay.at[c, 1, :, :, second_a], *sem, down_y)

    def by(c, k):
        def src(y_, half):
            return send_by.at[c, :, pl.ds(32 * y_ + OWN * half, OWN)]

        def dst(side, half):
            return recv_by.at[c, side, :, pl.ds(OWN * half, OWN)]

        sem = (by_s.at[c, k], by_r.at[c, k])
        if k == 0:
            return remote(src(y_far, 0), recv_bu.at[c, 0], *sem, up_y)
        if k == 1:
            return remote(src(y_far, 1), recv_bu.at[c, 1], *sem, down_y)
        if k == 2:
            return remote(src(y_next, 1), dst(0, 1), *sem, up_y)
        if k == 3:
            return remote(src(y_prev, 0), dst(1, 0), *sem, down_y)
        if k == 4:
            return remote(src(y_next, 0), dst(0, 0), *sem, up_y)
        return remote(src(y_prev, 1), dst(1, 1), *sem, down_y)

    def same(view, send, recv, device):
        return remote(view, view, send, recv, device)

    def gather_az(c, k, zl_):
        y_ = (y, y_prev, y_next, y_far)[k]
        view = delta_a.at[:, pl.ds(c * CHUNK + 64 * zl_ + OWN * y_, OWN)]
        return same(view, gaz_s.at[c, k], gaz_r.at[c, k], z_pair)

    def gather_bz(c, zl_):
        return same(delta_b.at[:, rows_b(c, y, OWN * zl_, OWN)], gbz_s.at[c], gbz_r.at[c], z_pair)

    def gather_ay(c, k, y_):
        sem = (gay_s.at[c, k], gay_r.at[c, k])
        rows = rows_a(c, y_)
        view = (delta_a.at[:, rows], delta_a.at[:, rows],
                delta_a.at[:, rows, second_a], delta_a.at[:, rows, first_a])[k]
        return same(view, *sem, down_y if k % 2 else up_y)

    def gather_by(c, k, y_):
        sem = (gby_s.at[c, k], gby_r.at[c, k])
        rows = (rows_b(c, y_, 0, 32), rows_b(c, y_, 0, 32), rows_b(c, y_, OWN, OWN), rows_b(c, y_, 0, OWN))[k]
        return same(delta_b.at[:, rows], *sem, down_y if k % 2 else up_y)

    def out_copies(c):
        rows = pl.ds(c * CHUNK, CHUNK)
        return (
            pltpu.make_async_copy(delta_a.at[:, rows], delta_out.at[:, rows, pl.ds(0, WIDTH_A)], out_sem.at[0, c]),
            pltpu.make_async_copy(delta_b.at[:, rows], delta_out.at[:, rows, pl.ds(WIDTH_A, WIDTH_B)], out_sem.at[1, c]),
        )

    tokens_copy = pltpu.make_async_copy(tok.at[:, pl.ds(LEAD, TOKENS)], tokens_out, load_sem.at[0])

    def partial_a(c):
        p = lax.rem(c, SLOTS)
        rows = pl.ds(LEAD + c * CHUNK, CHUNK)

        def send(i):
            send_az[c, i] = part_a[p, i, pl.ds(64 * (1 - zl), 64), :].astype(BF16)
            send_az_copy(c, i).start()

        act = tok[0, rows, :]
        part_a[p, 0] = dot_nn(act, wg[:, :WIDTH_A])
        send(0)
        part_a[p, 1] = dot_nn(act, wu[:, :WIDTH_A])
        send(1)

        @pl.when(c == 0)
        def _():
            loads[6].wait()
            first_tokens(1)

        part_a[p, 2] = dot_nt(tok[1, rows, :], wd[:WIDTH_A, :])
        send(2)

    def partial_b(c):
        p = lax.rem(c, SLOTS)
        rows = pl.ds(LEAD + c * CHUNK, CHUNK)
        act = tok[0, rows, :]
        part_b[p, 0] = dot_nn(act, wg[:, WIDTH_A:])
        part_b[p, 1] = dot_nn(act, wu[:, WIDTH_A:])
        part_b[p, 2] = dot_nt(tok[1, rows, :], wd[WIDTH_A:, :])
        for i in range(3):
            send_by[c, i] = part_b[p, i].astype(BF16)
        for k in range(4):
            by(c, k).start()

    def plane_a(c):
        p = lax.rem(c, SLOTS)
        plane = pl.ds(64 * zl, 64)
        for i in range(3):
            send_az_copy(c, i).wait_recv()
            total = part_a[p, i, plane, :] + recv_az[c, i].astype(F32)
            part_a[p, i, plane, :] = total
            send_ay[c, i] = total.astype(BF16)
        for k in range(4):
            ay(c, k).start()

    def ring_a(c):
        p = lax.rem(c, SLOTS)
        ay(c, 0).wait_recv()
        for i in range(3):
            total = part_a[p, i, pl.ds(64 * zl + OWN * y_next, OWN), :HALF_A] + recv_af[c, i].astype(F32)
            send_ay[c, i, pl.ds(OWN * y_next, OWN), :HALF_A] = total.astype(BF16)
        ay(c, 4).start()
        ay(c, 1).wait_recv()
        for i in range(3):
            total = part_a[p, i, pl.ds(64 * zl + OWN * y_prev, OWN), HALF_A:] + recv_as[c, i].astype(F32)
            send_ay[c, i, pl.ds(OWN * y_prev, OWN), HALF_A:] = total.astype(BF16)
        ay(c, 5).start()

    def ring_b(c):
        p = lax.rem(c, SLOTS)
        for side, y_ in ((0, y_next), (1, y_prev)):
            by(c, side).wait_recv()
            mine = pl.ds(32 * y_ + OWN * side, OWN)
            for i in range(3):
                total = part_b[p, i, mine, :] + recv_bu[c, side, i].astype(F32)
                send_by[c, i, mine, :] = total.astype(BF16)
            by(c, 4 + side).start()

    def own_a(c):
        p = lax.rem(c, SLOTS)
        for k in range(2, 6):
            ay(c, k).wait_recv()
        mine = pl.ds(64 * zl + OWN * y, OWN)
        sums = [
            part_a[p, i, mine, :] + recv_ay[c, 0, i].astype(F32) + recv_ay[c, 1, i].astype(F32)
            for i in range(3)
        ]
        for i, value in enumerate(swiglu_back(*sums)):
            delta_a[i, rows_a(c, y), :] = value
        for k in range(2):
            gather_ay(c, k, y).start()
        gather_az(c, 0, zl).start()

    def own_b(c):
        p = lax.rem(c, SLOTS)
        for k in range(2, 6):
            by(c, k).wait_recv()
        for half in range(2):
            mine = pl.ds(32 * y + OWN * half, OWN)
            for i in range(3):
                total = part_b[p, i, mine, :]
                for side in range(2):
                    total = total + recv_by[c, side, i, pl.ds(OWN * half, OWN), :].astype(F32)
                part_b[p, i, mine, :] = total
        for i in range(3):
            send_bz[c, i] = part_b[p, i, pl.ds(32 * y + OWN * (1 - zl), OWN), :].astype(BF16)
        send_bz_copy(c).start()

    def point_b(c):
        p = lax.rem(c, SLOTS)
        send_bz_copy(c).wait_recv()
        mine = pl.ds(32 * y + OWN * zl, OWN)
        sums = [part_b[p, i, mine, :] + recv_bz[c, i].astype(F32) for i in range(3)]
        for i, value in enumerate(swiglu_back(*sums)):
            delta_b[i, rows_b(c, y, OWN * zl, OWN), :] = value
        gather_bz(c, zl).start()

    def forward_a(c):
        gather_ay(c, 0, y_prev).wait_recv()
        gather_ay(c, 2, y_prev).start()
        gather_az(c, 1, zl).start()
        gather_ay(c, 1, y_next).wait_recv()
        gather_ay(c, 3, y_next).start()
        gather_az(c, 2, zl).start()

    def quarter_b(c):
        gather_bz(c, 1 - zl).wait_recv()
        for k in range(2):
            gather_by(c, k, y).start()

    def swap_a(c):
        for k in (2, 3):
            gather_ay(c, k, y_far).wait_recv()
        gather_az(c, 3, zl).start()

    def forward_b(c):
        gather_by(c, 0, y_prev).wait_recv()
        gather_by(c, 2, y_prev).start()
        gather_by(c, 1, y_next).wait_recv()
        gather_by(c, 3, y_next).start()

    def input_grad_a(c):
        rows, out = pl.ds(c * CHUNK, CHUNK), pl.ds(LEAD + c * CHUNK, CHUNK)
        for k in range(4):
            gather_az(c, k, 1 - zl).wait_recv()
        igrad[out, :] = dot_nt(delta_a[1, rows, :], wg[:, :WIDTH_A])
        igrad[out, :] += dot_nt(delta_a[2, rows, :], wu[:, :WIDTH_A])

    def input_grad_b(c):
        rows, out = pl.ds(c * CHUNK, CHUNK), pl.ds(LEAD + c * CHUNK, CHUNK)
        for k in (2, 3):
            gather_by(c, k, y_far).wait_recv()
        for copy in out_copies(c):
            copy.start()
        igrad[out, :] += dot_nt(delta_b[1, rows, :], wg[:, WIDTH_A:])
        igrad[out, :] += dot_nt(delta_b[2, rows, :], wu[:, WIDTH_A:])

    def core_copy(unit):
        src = igrad.at[pl.ds(at(unit, 1), BLOCK)]
        return remote(src, core_recv.at[unit], core_s.at[unit], core_r.at[unit], sibling)

    def x_copy(unit):
        src = igrad.at[pl.ds(at(unit, 0), BLOCK)]
        return remote(src, x_recv.at[unit - 1], x_s.at[unit - 1], x_r.at[unit - 1], at_x(unit_dist[unit]))

    def sum_core(unit):
        core_copy(unit).wait_recv()
        rows = pl.ds(at(unit, 0), BLOCK)
        igrad[rows, :] = igrad[rows, :] + core_recv[unit]
        x_copy(unit).start()

    stages = (
        (6, input_grad_a), (6, input_grad_b), (5, swap_a), (5, forward_b), (4, forward_a), (4, quarter_b),
        (3, own_a), (3, point_b), (2, ring_a), (2, own_b), (1, plane_a), (1, ring_b), (0, partial_a), (0, partial_b),
    )
    units_done = ((0,), (1,), (2, 3), (4,), (5, 6), (7,))
    units_wait = ((), (1,), (2, 3), (4, 5), (6,), (7,))
    units_pass = ((3, 7), (4, 5), (6,))

    first = [stage for delay, stage in stages if delay == 0][0]
    last = max(delay for delay, _ in stages)

    @pl.loop(0, CHUNKS + last)
    def _(t):
        for delay, stage in stages:
            if stage is first:
                for c in range(1, CHUNKS):
                    @pl.when(t == c)
                    def _():
                        for unit in units_wait[c]:
                            for i in range(2):
                                to_sibling(i, unit).wait_recv()

            if stage is input_grad_a:
                for c in range(CHUNKS - 1):
                    @pl.when(t == c + last + 1)
                    def _():
                        for unit in units_done[c]:
                            if unit:
                                sum_core(unit)

            @pl.when((t >= delay) & (t < CHUNKS + delay))
            def _():
                stage(t - delay)

            if stage is input_grad_b:
                for c in range(CHUNKS):
                    @pl.when(t == c + last)
                    def _():
                        for unit in units_done[c]:
                            core_copy(unit).start()

        for c, units in enumerate(units_pass):
            @pl.when(t == c)
            def _():
                for unit in units:
                    for i in range(2):
                        pass_on(i, unit)

        @pl.when(t == CHUNKS - 1)
        def _():
            tokens_copy.start()

    core_copy(0).wait_recv()
    near = igrad[pl.ds(at(0, 0) + LEAD, BLOCK - LEAD), :], igrad[again, :]
    near = jnp.concatenate([near[1], near[0]], axis=0) + core_recv[0]
    for unit in (1, 2, 3):
        x_copy(unit).wait_recv()
        near = near + x_recv[unit - 1]
    near_out[...] = near
    core_copy(7).wait_recv()
    other = igrad[pl.ds(at(7, 0), BLOCK), :] + core_recv[7]
    for unit in (4, 5, 6):
        x_copy(unit).wait_recv()
        other = other + x_recv[unit - 1]
    other_out[...] = other

    for i in range(2):
        to_zh(i).wait_send()
        for other_, dist in to_unit:
            to_x(i, other_, dist).wait_send()
        for unit in range(8):
            to_sibling(i, unit).wait_send()
    for unit in range(8):
        core_copy(unit).wait_send()
    for unit in range(1, 7):
        x_copy(unit).wait_send()

    @pl.loop(0, CHUNKS)
    def _(c):
        for i in range(3):
            send_az_copy(c, i).wait_send()
        send_bz_copy(c).wait_send()
        for k in range(4):
            gather_az(c, k, zl).wait_send()
        gather_bz(c, zl).wait_send()
        for k in range(6):
            ay(c, k).wait_send()
            by(c, k).wait_send()
        for k in range(4):
            gather_ay(c, k, y).wait_send()
            gather_by(c, k, y).wait_send()
        for copy in out_copies(c):
            copy.wait()

    tokens_copy.wait()


def exchange(activations, out_grad, w_gate, w_up, w_down):
    dma = pltpu.SemaphoreType.DMA
    any_spec = pl.BlockSpec(memory_space=pl.ANY)
    vmem_spec = pl.BlockSpec(memory_space=pltpu.VMEM)
    n = CHUNKS
    return pl.pallas_call(
        exchange_kernel,
        out_shape=[
            jax.ShapeDtypeStruct((2, TOKENS, D_LOCAL), BF16),
            jax.ShapeDtypeStruct((3, TOKENS, H_LOCAL), BF16),
            *[jax.ShapeDtypeStruct((BLOCK, D_LOCAL), F32)] * 2,
        ],
        in_specs=[any_spec] * 5,
        out_specs=[any_spec] * 2 + [vmem_spec] * 2,
        scratch_shapes=[
            pltpu.VMEM((D_LOCAL, H_LOCAL), BF16),
            pltpu.VMEM((D_LOCAL, H_LOCAL), BF16),
            pltpu.VMEM((H_LOCAL, D_LOCAL), BF16),
            pltpu.VMEM((2, TOKENS + LEAD, D_LOCAL), BF16),
            pltpu.VMEM((SLOTS, 3, CHUNK, WIDTH_A), F32),
            pltpu.VMEM((SLOTS, 3, CHUNK, WIDTH_B), F32),
            pltpu.VMEM((n, 3, 64, WIDTH_A), BF16),
            pltpu.VMEM((n, 3, 64, WIDTH_A), BF16),
            pltpu.VMEM((n, 3, 64, WIDTH_A), BF16),
            pltpu.VMEM((n, 3, OWN, HALF_A), BF16),
            pltpu.VMEM((n, 3, OWN, WIDTH_A - HALF_A), BF16),
            pltpu.VMEM((n, 2, 3, OWN, WIDTH_A), BF16),
            pltpu.VMEM((n, 3, CHUNK, WIDTH_B), BF16),
            pltpu.VMEM((n, 2, 3, OWN, WIDTH_B), BF16),
            pltpu.VMEM((n, 2, 3, 32, WIDTH_B), BF16),
            pltpu.VMEM((n, 3, OWN, WIDTH_B), BF16),
            pltpu.VMEM((n, 3, OWN, WIDTH_B), BF16),
            pltpu.VMEM((3, TOKENS, WIDTH_A), BF16),
            pltpu.VMEM((3, TOKENS, WIDTH_B), BF16),
            pltpu.VMEM((TOKENS + LEAD, D_LOCAL), F32),
            pltpu.VMEM((8, BLOCK, D_LOCAL), F32),
            pltpu.VMEM((6, BLOCK, D_LOCAL), F32),
            dma((7,)), dma((2,)), dma((2,)), dma((2, 8)), dma((2, 8)), dma((2, 6)), dma((2, 6)),
            dma((n, 3)), dma((n, 3)), dma((n,)), dma((n,)), dma((n, 4)), dma((n, 4)), dma((n,)), dma((n,)),
            dma((n, 6)), dma((n, 6)), dma((n, 6)), dma((n, 6)),
            dma((n, 4)), dma((n, 4)), dma((n, 4)), dma((n, 4)),
            dma((8,)), dma((8,)), dma((6,)), dma((6,)),
            dma((2, n)),
        ],
        compiler_params=pltpu.CompilerParams(
            collective_id=0, has_side_effects=True, vmem_limit_bytes=60 * 2**20
        ),
        cost_estimate=pl.CostEstimate(
            flops=10 * TOKENS * D_LOCAL * H_LOCAL, bytes_accessed=22 * 2**20, transcendentals=0
        ),
        name="exchange",
    )(activations, out_grad, w_gate, w_up, w_down)


def weights_kernel(
    tok_in, delta_in, gate_out, up_out, down_out,
    tok, delta, gate, up, down, in_sem, out_sem,
):
    loads = [
        pltpu.make_async_copy(tok_in.at[0], tok.at[0], in_sem.at[0]),
        pltpu.make_async_copy(delta_in.at[1], delta.at[1], in_sem.at[1]),
        pltpu.make_async_copy(delta_in.at[2], delta.at[2], in_sem.at[2]),
        pltpu.make_async_copy(delta_in.at[0], delta.at[0], in_sem.at[3]),
        pltpu.make_async_copy(tok_in.at[1], tok.at[1], in_sem.at[4]),
    ]
    for load in loads:
        load.start()
    stores = []

    def store(src, dst, start, size):
        copy = pltpu.make_async_copy(
            src.at[pl.ds(start, size)], dst.at[pl.ds(start, size)], out_sem.at[len(stores)]
        )
        copy.start()
        stores.append(copy)

    loads[0].wait()
    for load, i, buf, out in ((loads[1], 1, gate, gate_out), (loads[2], 2, up, up_out)):
        load.wait()
        for m in range(0, D_LOCAL, 256):
            buf[m : m + 256, :] = dot_tn(tok[0, :, m : m + 256], delta[i]).astype(BF16)
            store(buf, out, m, 256)
    loads[3].wait()
    loads[4].wait()
    for m in range(0, H_LOCAL, 256):
        size = min(256, H_LOCAL - m)
        down[m : m + size, :] = dot_tn(delta[0, :, m : m + size], tok[1]).astype(BF16)
        store(down, down_out, m, size)
    for copy in stores:
        copy.wait()


def weight_grads(tokens, deltas):
    any_spec = pl.BlockSpec(memory_space=pl.ANY)
    shapes = [(D_LOCAL, H_LOCAL), (D_LOCAL, H_LOCAL), (H_LOCAL, D_LOCAL)]
    return pl.pallas_call(
        weights_kernel,
        out_shape=[jax.ShapeDtypeStruct(s, BF16) for s in shapes],
        in_specs=[any_spec] * 2,
        out_specs=[any_spec] * 3,
        scratch_shapes=[
            pltpu.VMEM((2, TOKENS, D_LOCAL), BF16),
            pltpu.VMEM((3, TOKENS, H_LOCAL), BF16),
            *[pltpu.VMEM(s, BF16) for s in shapes],
            pltpu.SemaphoreType.DMA((5,)),
            pltpu.SemaphoreType.DMA((15,)),
        ],
        compiler_params=pltpu.CompilerParams(vmem_limit_bytes=56 * 2**20),
        cost_estimate=pl.CostEstimate(
            flops=6 * TOKENS * D_LOCAL * H_LOCAL, bytes_accessed=22 * 2**20, transcendentals=0
        ),
        name="weight_grads",
    )(tokens, deltas)


def per_device(activations, out_grad, w_gate, w_up, w_down):
    tokens, deltas, near, other = exchange(activations, out_grad, w_gate, w_up, w_down)
    other = lax.ppermute(other, "col", [(c, (c + 8) % 16) for c in range(16)])
    gate_grad, up_grad, down_grad = weight_grads(tokens, deltas)
    return (near + other).astype(BF16), gate_grad, up_grad, down_grad


def solution(mesh):
    placed = (P("col", "row"), P("col", "row"), P("row", "col"), P("row", "col"), P("col", "row"))
    return jax.shard_map(
        per_device,
        mesh=mesh,
        in_specs=placed,
        out_specs=(P("col", "row"), P("row", "col"), P("row", "col"), P("col", "row")),
        check_vma=False,
    )
```

```python
import functools

import jax
import jax.numpy as jnp
from jax import lax
from jax.experimental import pallas as pl
from jax.experimental.pallas import tpu as pltpu
from jax.sharding import PartitionSpec as P

F32 = jnp.float32
BF16 = jnp.bfloat16
MESH = pl.DeviceIdType.MESH

CHUNKS = 6
CHUNK = 128
OWN = 16
SLOTS = 4
D_LOCAL = 1024
H_LOCAL = 1664
TOKENS = 768
BLOCK = 48
WIDTH_A = 768
HALF_A = 384
WIDTH_B = H_LOCAL - WIDTH_A
LEAD = 32
BLOCK_ORDER = (
    (0, 0), (0, 1), (1, 0), (2, 0), (3, 0), (1, 1), (2, 1), (3, 1),
    (4, 0), (4, 1), (5, 0), (5, 1), (6, 0), (6, 1), (7, 0), (7, 1),
)


def dot_nn(a, b):
    return jnp.dot(a, b, preferred_element_type=F32)


def dot_nt(a, b):
    return lax.dot_general(a, b, (((1,), (1,)), ((), ())), preferred_element_type=F32)


def dot_tn(a, b):
    return lax.dot_general(a, b, (((0,), (0,)), ((), ())), preferred_element_type=F32)


def swiglu_back(gate, upper, hidden_grad):
    sig = jax.nn.sigmoid(gate)
    act = gate * sig
    hidden = (act * upper).astype(BF16)
    gate_delta = (hidden_grad * upper * sig * (1.0 + gate * (1.0 - sig))).astype(BF16)
    up_delta = (hidden_grad * act).astype(BF16)
    return hidden, gate_delta, up_delta


def exchange_kernel(
    act_in, grad_in, wg_in, wu_in, wd_in,
    tokens_out, delta_out, near_out, other_out,
    wg, wu, wd, tok, part_a, part_b,
    send_az, recv_az, send_ay, recv_af, recv_as, recv_ay,
    send_by, recv_bu, recv_by, send_bz, recv_bz,
    delta_a, delta_b, igrad, core_recv, x_recv,
    load_sem, zh_s, zh_r, sib_s, sib_r, tokx_s, tokx_r,
    az_s, az_r, bz_s, bz_r, gaz_s, gaz_r, gbz_s, gbz_r,
    ay_s, ay_r, by_s, by_r, gay_s, gay_r, gby_s, gby_r,
    core_s, core_r, x_s, x_r, out_sem,
):
    row = lax.axis_index("row")
    col = lax.axis_index("col")
    y = lax.rem(row, 4)
    zl = lax.div(row, 4)
    zh = lax.div(col, 8)
    x = lax.rem(lax.div(col, 2), 4)
    core = lax.rem(col, 2)
    y_next, y_prev, y_far = lax.rem(y + 1, 4), lax.rem(y + 3, 4), lax.rem(y + 2, 4)

    def at_x(dist):
        return (row, zh * 8 + lax.rem(x + dist, 4) * 2 + core)

    up_y = (zl * 4 + y_next, col)
    down_y = (zl * 4 + y_prev, col)
    z_pair = ((1 - zl) * 4 + y, col)
    zh_pair = (row, (1 - zh) * 8 + x * 2 + core)
    sibling = (row, zh * 8 + x * 2 + 1 - core)
    partners = [up_y, down_y, z_pair, at_x(1), at_x(2), at_x(3), zh_pair, sibling]

    def remote(src, dst, send, recv, device):
        return pltpu.make_async_remote_copy(
            src_ref=src, dst_ref=dst, send_sem=send, recv_sem=recv,
            device_id=device, device_id_type=MESH,
        )

    unit_dist = (0, 1, 3, 2, 2, 1, 3, 0)
    to_unit = {(0, 3): 1, (0, 1): 2, (0, 2): 3, (1, 2): 4, (1, 3): 5, (1, 1): 6}

    def at(unit, other_core):
        return BLOCK * BLOCK_ORDER.index((unit, other_core))

    def blk(i, unit, other_core):
        return tok.at[i, pl.ds(at(unit, other_core), BLOCK)]

    def to_zh(i):
        return remote(blk(i, 0, 0), blk(i, 7, 0), zh_s.at[i], zh_r.at[i], zh_pair)

    def to_sibling(i, unit):
        return remote(blk(i, unit, 0), blk(i, unit, 1), sib_s.at[i, unit], sib_r.at[i, unit], sibling)

    def to_x(i, other, dist):
        unit = to_unit[other, dist]
        return remote(blk(i, 7 * other, 0), blk(i, unit, 0), tokx_s.at[i, unit - 1], tokx_r.at[i, unit - 1], at_x(dist))

    def pass_on(i, unit):
        if unit == 7:
            to_zh(i).wait_recv()
            for dist in (2, 3, 1):
                to_x(i, 1, dist).start()
        else:
            view = blk(i, unit, 0)
            remote(view, view, tokx_s.at[i, unit - 1], tokx_r.at[i, unit - 1], at_x(unit_dist[unit])).wait_recv()
        to_sibling(i, unit).start()

    again = pl.ds(TOKENS, LEAD)
    loads = [
        pltpu.make_async_copy(act_in, tok.at[0, pl.ds(0, BLOCK)], load_sem.at[0]),
        pltpu.make_async_copy(grad_in, tok.at[1, pl.ds(0, BLOCK)], load_sem.at[1]),
        pltpu.make_async_copy(act_in.at[pl.ds(0, LEAD)], tok.at[0, again], load_sem.at[2]),
        pltpu.make_async_copy(grad_in.at[pl.ds(0, LEAD)], tok.at[1, again], load_sem.at[3]),
        pltpu.make_async_copy(wg_in, wg, load_sem.at[4]),
        pltpu.make_async_copy(wu_in, wu, load_sem.at[5]),
        pltpu.make_async_copy(wd_in, wd, load_sem.at[6]),
    ]
    barrier = pltpu.get_barrier_semaphore()
    for device in partners:
        pl.semaphore_signal(barrier, inc=1, device_id=device, device_id_type=MESH)
    for load in loads:
        load.start()
    pl.semaphore_wait(barrier, len(partners))

    loads[0].wait()
    loads[1].wait()
    for i in range(2):
        to_x(i, 0, 3).start()
        to_x(i, 0, 1).start()
        to_sibling(i, 0).start()
    for i in range(2):
        to_zh(i).start()
        to_x(i, 0, 2).start()

    def first_tokens(i):
        to_sibling(i, 0).wait_recv()
        pass_on(i, 1)
        pass_on(i, 2)

    for load in loads[2:6]:
        load.wait()
    first_tokens(0)

    def rows_a(c, y_):
        return pl.ds(c * CHUNK + 64 * zl + OWN * y_, OWN)

    def rows_b(c, y_, first, size):
        return pl.ds(c * CHUNK + 32 * y_ + first, size)

    first_a, second_a = pl.ds(0, HALF_A), pl.ds(HALF_A, WIDTH_A - HALF_A)

    def send_az_copy(c, i):
        return remote(send_az.at[c, i], recv_az.at[c, i], az_s.at[c, i], az_r.at[c, i], z_pair)

    def send_bz_copy(c):
        return remote(send_bz.at[c], recv_bz.at[c], bz_s.at[c], bz_r.at[c], z_pair)

    def ay(c, k):
        def src(y_, cols):
            return send_ay.at[c, :, pl.ds(OWN * y_, OWN), cols]

        sem = (ay_s.at[c, k], ay_r.at[c, k])
        if k == 0:
            return remote(src(y_far, first_a), recv_af.at[c], *sem, up_y)
        if k == 1:
            return remote(src(y_far, second_a), recv_as.at[c], *sem, down_y)
        if k == 2:
            return remote(src(y_next, second_a), recv_ay.at[c, 0, :, :, second_a], *sem, up_y)
        if k == 3:
            return remote(src(y_prev, first_a), recv_ay.at[c, 1, :, :, first_a], *sem, down_y)
        if k == 4:
            return remote(src(y_next, first_a), recv_ay.at[c, 0, :, :, first_a], *sem, up_y)
        return remote(src(y_prev, second_a), recv_ay.at[c, 1, :, :, second_a], *sem, down_y)

    def by(c, k):
        def src(y_, half):
            return send_by.at[c, :, pl.ds(32 * y_ + OWN * half, OWN)]

        def dst(side, half):
            return recv_by.at[c, side, :, pl.ds(OWN * half, OWN)]

        sem = (by_s.at[c, k], by_r.at[c, k])
        if k == 0:
            return remote(src(y_far, 0), recv_bu.at[c, 0], *sem, up_y)
        if k == 1:
            return remote(src(y_far, 1), recv_bu.at[c, 1], *sem, down_y)
        if k == 2:
            return remote(src(y_next, 1), dst(0, 1), *sem, up_y)
        if k == 3:
            return remote(src(y_prev, 0), dst(1, 0), *sem, down_y)
        if k == 4:
            return remote(src(y_next, 0), dst(0, 0), *sem, up_y)
        return remote(src(y_prev, 1), dst(1, 1), *sem, down_y)

    def same(view, send, recv, device):
        return remote(view, view, send, recv, device)

    def gather_az(c, k, zl_):
        y_ = (y, y_prev, y_next, y_far)[k]
        view = delta_a.at[:, pl.ds(c * CHUNK + 64 * zl_ + OWN * y_, OWN)]
        return same(view, gaz_s.at[c, k], gaz_r.at[c, k], z_pair)

    def gather_bz(c, zl_):
        return same(delta_b.at[:, rows_b(c, y, OWN * zl_, OWN)], gbz_s.at[c], gbz_r.at[c], z_pair)

    def gather_ay(c, k, y_):
        sem = (gay_s.at[c, k], gay_r.at[c, k])
        rows = rows_a(c, y_)
        view = (delta_a.at[:, rows], delta_a.at[:, rows],
                delta_a.at[:, rows, second_a], delta_a.at[:, rows, first_a])[k]
        return same(view, *sem, down_y if k % 2 else up_y)

    def gather_by(c, k, y_):
        sem = (gby_s.at[c, k], gby_r.at[c, k])
        mine, pair = rows_b(c, y_, OWN * zl, OWN), rows_b(c, y_, OWN * (1 - zl), OWN)
        rows = (mine, mine, rows_b(c, y_, OWN, OWN), rows_b(c, y_, 0, OWN), pair, pair)[k]
        return same(delta_b.at[:, rows], *sem, down_y if k % 2 else up_y)

    def out_copies(c):
        rows = pl.ds(c * CHUNK, CHUNK)
        return (
            pltpu.make_async_copy(delta_a.at[:, rows], delta_out.at[:, rows, pl.ds(0, WIDTH_A)], out_sem.at[0, c]),
            pltpu.make_async_copy(delta_b.at[:, rows], delta_out.at[:, rows, pl.ds(WIDTH_A, WIDTH_B)], out_sem.at[1, c]),
        )

    tokens_copy = pltpu.make_async_copy(tok.at[:, pl.ds(LEAD, TOKENS)], tokens_out, load_sem.at[0])

    def partial_a(c):
        p = lax.rem(c, SLOTS)
        rows = pl.ds(LEAD + c * CHUNK, CHUNK)

        def send(i):
            send_az[c, i] = part_a[p, i, pl.ds(64 * (1 - zl), 64), :].astype(BF16)
            send_az_copy(c, i).start()

        act = tok[0, rows, :]
        part_a[p, 0] = dot_nn(act, wg[:, :WIDTH_A])
        send(0)
        part_a[p, 1] = dot_nn(act, wu[:, :WIDTH_A])
        send(1)

        @pl.when(c == 0)
        def _():
            loads[6].wait()
            first_tokens(1)

        part_a[p, 2] = dot_nt(tok[1, rows, :], wd[:WIDTH_A, :])
        send(2)

    def partial_b(c):
        p = lax.rem(c, SLOTS)
        rows = pl.ds(LEAD + c * CHUNK, CHUNK)
        act = tok[0, rows, :]
        part_b[p, 0] = dot_nn(act, wg[:, WIDTH_A:])
        part_b[p, 1] = dot_nn(act, wu[:, WIDTH_A:])
        part_b[p, 2] = dot_nt(tok[1, rows, :], wd[WIDTH_A:, :])
        for i in range(3):
            send_by[c, i] = part_b[p, i].astype(BF16)
        for k in range(4):
            by(c, k).start()

    def plane_a(c):
        p = lax.rem(c, SLOTS)
        plane = pl.ds(64 * zl, 64)
        for i in range(3):
            send_az_copy(c, i).wait_recv()
            total = part_a[p, i, plane, :] + recv_az[c, i].astype(F32)
            part_a[p, i, plane, :] = total
            send_ay[c, i] = total.astype(BF16)
        for k in range(4):
            ay(c, k).start()

    def ring_a(c):
        p = lax.rem(c, SLOTS)
        ay(c, 0).wait_recv()
        for i in range(3):
            total = part_a[p, i, pl.ds(64 * zl + OWN * y_next, OWN), :HALF_A] + recv_af[c, i].astype(F32)
            send_ay[c, i, pl.ds(OWN * y_next, OWN), :HALF_A] = total.astype(BF16)
        ay(c, 4).start()
        ay(c, 1).wait_recv()
        for i in range(3):
            total = part_a[p, i, pl.ds(64 * zl + OWN * y_prev, OWN), HALF_A:] + recv_as[c, i].astype(F32)
            send_ay[c, i, pl.ds(OWN * y_prev, OWN), HALF_A:] = total.astype(BF16)
        ay(c, 5).start()

    def ring_b(c):
        p = lax.rem(c, SLOTS)
        for side, y_ in ((0, y_next), (1, y_prev)):
            by(c, side).wait_recv()
            mine = pl.ds(32 * y_ + OWN * side, OWN)
            for i in range(3):
                total = part_b[p, i, mine, :] + recv_bu[c, side, i].astype(F32)
                send_by[c, i, mine, :] = total.astype(BF16)
            by(c, 4 + side).start()

    def own_a(c):
        p = lax.rem(c, SLOTS)
        for k in range(2, 6):
            ay(c, k).wait_recv()
        mine = pl.ds(64 * zl + OWN * y, OWN)
        sums = [
            part_a[p, i, mine, :] + recv_ay[c, 0, i].astype(F32) + recv_ay[c, 1, i].astype(F32)
            for i in range(3)
        ]
        for i, value in enumerate(swiglu_back(*sums)):
            delta_a[i, rows_a(c, y), :] = value
        for k in range(2):
            gather_ay(c, k, y).start()
        gather_az(c, 0, zl).start()

    def own_b(c):
        p = lax.rem(c, SLOTS)
        for k in range(2, 6):
            by(c, k).wait_recv()
        for half in range(2):
            mine = pl.ds(32 * y + OWN * half, OWN)
            for i in range(3):
                total = part_b[p, i, mine, :]
                for side in range(2):
                    total = total + recv_by[c, side, i, pl.ds(OWN * half, OWN), :].astype(F32)
                part_b[p, i, mine, :] = total
        for i in range(3):
            send_bz[c, i] = part_b[p, i, pl.ds(32 * y + OWN * (1 - zl), OWN), :].astype(BF16)
        send_bz_copy(c).start()

    def point_b(c):
        p = lax.rem(c, SLOTS)
        send_bz_copy(c).wait_recv()
        mine = pl.ds(32 * y + OWN * zl, OWN)
        sums = [part_b[p, i, mine, :] + recv_bz[c, i].astype(F32) for i in range(3)]
        for i, value in enumerate(swiglu_back(*sums)):
            delta_b[i, rows_b(c, y, OWN * zl, OWN), :] = value
        gather_bz(c, zl).start()
        for k in range(2):
            gather_by(c, k, y).start()

    def forward_a(c):
        gather_ay(c, 0, y_prev).wait_recv()
        gather_ay(c, 2, y_prev).start()
        gather_az(c, 1, zl).start()
        gather_ay(c, 1, y_next).wait_recv()
        gather_ay(c, 3, y_next).start()
        gather_az(c, 2, zl).start()

    def quarter_b(c):
        gather_bz(c, 1 - zl).wait_recv()
        for k in (4, 5):
            gather_by(c, k, y).start()

    def swap_a(c):
        for k in (2, 3):
            gather_ay(c, k, y_far).wait_recv()
        gather_az(c, 3, zl).start()

    def forward_b(c):
        for k in (0, 4):
            gather_by(c, k, y_prev).wait_recv()
        gather_by(c, 2, y_prev).start()
        for k in (1, 5):
            gather_by(c, k, y_next).wait_recv()
        gather_by(c, 3, y_next).start()

    def input_grad_a(c):
        rows, out = pl.ds(c * CHUNK, CHUNK), pl.ds(LEAD + c * CHUNK, CHUNK)
        for k in range(4):
            gather_az(c, k, 1 - zl).wait_recv()
        igrad[out, :] = dot_nt(delta_a[1, rows, :], wg[:, :WIDTH_A])
        igrad[out, :] += dot_nt(delta_a[2, rows, :], wu[:, :WIDTH_A])

    def input_grad_b(c):
        rows, out = pl.ds(c * CHUNK, CHUNK), pl.ds(LEAD + c * CHUNK, CHUNK)
        for k in (2, 3):
            gather_by(c, k, y_far).wait_recv()
        for copy in out_copies(c):
            copy.start()
        igrad[out, :] += dot_nt(delta_b[1, rows, :], wg[:, WIDTH_A:])
        igrad[out, :] += dot_nt(delta_b[2, rows, :], wu[:, WIDTH_A:])

    def core_copy(unit):
        src = igrad.at[pl.ds(at(unit, 1), BLOCK)]
        return remote(src, core_recv.at[unit], core_s.at[unit], core_r.at[unit], sibling)

    def x_copy(unit):
        src = igrad.at[pl.ds(at(unit, 0), BLOCK)]
        return remote(src, x_recv.at[unit - 1], x_s.at[unit - 1], x_r.at[unit - 1], at_x(unit_dist[unit]))

    def sum_core(unit):
        core_copy(unit).wait_recv()
        rows = pl.ds(at(unit, 0), BLOCK)
        igrad[rows, :] = igrad[rows, :] + core_recv[unit]
        x_copy(unit).start()

    stages = (
        (6, input_grad_a), (6, input_grad_b), (5, swap_a), (5, forward_b), (4, forward_a), (4, quarter_b),
        (3, own_a), (3, point_b), (2, ring_a), (2, own_b), (1, plane_a), (1, ring_b), (0, partial_a), (0, partial_b),
    )
    units_done = ((0,), (1,), (2, 3), (4,), (5, 6), (7,))
    units_wait = ((), (1,), (2, 3), (4, 5), (6,), (7,))
    units_pass = ((3, 7), (4, 5), (6,))

    first = [stage for delay, stage in stages if delay == 0][0]
    last = max(delay for delay, _ in stages)

    @pl.loop(0, CHUNKS + last)
    def _(t):
        for delay, stage in stages:
            if stage is first:
                for c in range(1, CHUNKS):
                    @pl.when(t == c)
                    def _():
                        for unit in units_wait[c]:
                            for i in range(2):
                                to_sibling(i, unit).wait_recv()

            if stage is input_grad_a:
                for c in range(CHUNKS - 1):
                    @pl.when(t == c + last + 1)
                    def _():
                        for unit in units_done[c]:
                            if unit:
                                sum_core(unit)

            @pl.when((t >= delay) & (t < CHUNKS + delay))
            def _():
                stage(t - delay)

            if stage is input_grad_b:
                for c in range(CHUNKS):
                    @pl.when(t == c + last)
                    def _():
                        for unit in units_done[c]:
                            core_copy(unit).start()

        for c, units in enumerate(units_pass):
            @pl.when(t == c)
            def _():
                for unit in units:
                    for i in range(2):
                        pass_on(i, unit)

        @pl.when(t == CHUNKS - 1)
        def _():
            tokens_copy.start()

    core_copy(0).wait_recv()
    near = igrad[pl.ds(at(0, 0) + LEAD, BLOCK - LEAD), :], igrad[again, :]
    near = jnp.concatenate([near[1], near[0]], axis=0) + core_recv[0]
    for unit in (1, 2, 3):
        x_copy(unit).wait_recv()
        near = near + x_recv[unit - 1]
    near_out[...] = near
    core_copy(7).wait_recv()
    other = igrad[pl.ds(at(7, 0), BLOCK), :] + core_recv[7]
    for unit in (4, 5, 6):
        x_copy(unit).wait_recv()
        other = other + x_recv[unit - 1]
    other_out[...] = other

    for i in range(2):
        to_zh(i).wait_send()
        for other_, dist in to_unit:
            to_x(i, other_, dist).wait_send()
        for unit in range(8):
            to_sibling(i, unit).wait_send()
    for unit in range(8):
        core_copy(unit).wait_send()
    for unit in range(1, 7):
        x_copy(unit).wait_send()

    @pl.loop(0, CHUNKS)
    def _(c):
        for i in range(3):
            send_az_copy(c, i).wait_send()
        send_bz_copy(c).wait_send()
        for k in range(4):
            gather_az(c, k, zl).wait_send()
        gather_bz(c, zl).wait_send()
        for k in range(6):
            ay(c, k).wait_send()
            by(c, k).wait_send()
        for k in range(4):
            gather_ay(c, k, y).wait_send()
        for k in range(6):
            gather_by(c, k, y).wait_send()
        for copy in out_copies(c):
            copy.wait()

    tokens_copy.wait()


def exchange(activations, out_grad, w_gate, w_up, w_down):
    dma = pltpu.SemaphoreType.DMA
    any_spec = pl.BlockSpec(memory_space=pl.ANY)
    vmem_spec = pl.BlockSpec(memory_space=pltpu.VMEM)
    n = CHUNKS
    return pl.pallas_call(
        exchange_kernel,
        out_shape=[
            jax.ShapeDtypeStruct((2, TOKENS, D_LOCAL), BF16),
            jax.ShapeDtypeStruct((3, TOKENS, H_LOCAL), BF16),
            *[jax.ShapeDtypeStruct((BLOCK, D_LOCAL), F32)] * 2,
        ],
        in_specs=[any_spec] * 5,
        out_specs=[any_spec] * 2 + [vmem_spec] * 2,
        scratch_shapes=[
            pltpu.VMEM((D_LOCAL, H_LOCAL), BF16),
            pltpu.VMEM((D_LOCAL, H_LOCAL), BF16),
            pltpu.VMEM((H_LOCAL, D_LOCAL), BF16),
            pltpu.VMEM((2, TOKENS + LEAD, D_LOCAL), BF16),
            pltpu.VMEM((SLOTS, 3, CHUNK, WIDTH_A), F32),
            pltpu.VMEM((SLOTS, 3, CHUNK, WIDTH_B), F32),
            pltpu.VMEM((n, 3, 64, WIDTH_A), BF16),
            pltpu.VMEM((n, 3, 64, WIDTH_A), BF16),
            pltpu.VMEM((n, 3, 64, WIDTH_A), BF16),
            pltpu.VMEM((n, 3, OWN, HALF_A), BF16),
            pltpu.VMEM((n, 3, OWN, WIDTH_A - HALF_A), BF16),
            pltpu.VMEM((n, 2, 3, OWN, WIDTH_A), BF16),
            pltpu.VMEM((n, 3, CHUNK, WIDTH_B), BF16),
            pltpu.VMEM((n, 2, 3, OWN, WIDTH_B), BF16),
            pltpu.VMEM((n, 2, 3, 32, WIDTH_B), BF16),
            pltpu.VMEM((n, 3, OWN, WIDTH_B), BF16),
            pltpu.VMEM((n, 3, OWN, WIDTH_B), BF16),
            pltpu.VMEM((3, TOKENS, WIDTH_A), BF16),
            pltpu.VMEM((3, TOKENS, WIDTH_B), BF16),
            pltpu.VMEM((TOKENS + LEAD, D_LOCAL), F32),
            pltpu.VMEM((8, BLOCK, D_LOCAL), F32),
            pltpu.VMEM((6, BLOCK, D_LOCAL), F32),
            dma((7,)), dma((2,)), dma((2,)), dma((2, 8)), dma((2, 8)), dma((2, 6)), dma((2, 6)),
            dma((n, 3)), dma((n, 3)), dma((n,)), dma((n,)), dma((n, 4)), dma((n, 4)), dma((n,)), dma((n,)),
            dma((n, 6)), dma((n, 6)), dma((n, 6)), dma((n, 6)),
            dma((n, 4)), dma((n, 4)), dma((n, 6)), dma((n, 6)),
            dma((8,)), dma((8,)), dma((6,)), dma((6,)),
            dma((2, n)),
        ],
        compiler_params=pltpu.CompilerParams(
            collective_id=0, has_side_effects=True, vmem_limit_bytes=60 * 2**20
        ),
        cost_estimate=pl.CostEstimate(
            flops=10 * TOKENS * D_LOCAL * H_LOCAL, bytes_accessed=22 * 2**20, transcendentals=0
        ),
        name="exchange",
    )(activations, out_grad, w_gate, w_up, w_down)


def weights_kernel(
    tok_in, delta_in, gate_out, up_out, down_out,
    tok, delta, gate, up, down, in_sem, out_sem,
):
    loads = [
        pltpu.make_async_copy(tok_in.at[0], tok.at[0], in_sem.at[0]),
        pltpu.make_async_copy(delta_in.at[1], delta.at[1], in_sem.at[1]),
        pltpu.make_async_copy(delta_in.at[2], delta.at[2], in_sem.at[2]),
        pltpu.make_async_copy(delta_in.at[0], delta.at[0], in_sem.at[3]),
        pltpu.make_async_copy(tok_in.at[1], tok.at[1], in_sem.at[4]),
    ]
    for load in loads:
        load.start()
    stores = []

    def store(src, dst, start, size):
        copy = pltpu.make_async_copy(
            src.at[pl.ds(start, size)], dst.at[pl.ds(start, size)], out_sem.at[len(stores)]
        )
        copy.start()
        stores.append(copy)

    loads[0].wait()
    for load, i, buf, out in ((loads[1], 1, gate, gate_out), (loads[2], 2, up, up_out)):
        load.wait()
        for m in range(0, D_LOCAL, 256):
            buf[m : m + 256, :] = dot_tn(tok[0, :, m : m + 256], delta[i]).astype(BF16)
            store(buf, out, m, 256)
    loads[3].wait()
    loads[4].wait()
    for m in range(0, H_LOCAL, 256):
        size = min(256, H_LOCAL - m)
        down[m : m + size, :] = dot_tn(delta[0, :, m : m + size], tok[1]).astype(BF16)
        store(down, down_out, m, size)
    for copy in stores:
        copy.wait()


def weight_grads(tokens, deltas):
    any_spec = pl.BlockSpec(memory_space=pl.ANY)
    shapes = [(D_LOCAL, H_LOCAL), (D_LOCAL, H_LOCAL), (H_LOCAL, D_LOCAL)]
    return pl.pallas_call(
        weights_kernel,
        out_shape=[jax.ShapeDtypeStruct(s, BF16) for s in shapes],
        in_specs=[any_spec] * 2,
        out_specs=[any_spec] * 3,
        scratch_shapes=[
            pltpu.VMEM((2, TOKENS, D_LOCAL), BF16),
            pltpu.VMEM((3, TOKENS, H_LOCAL), BF16),
            *[pltpu.VMEM(s, BF16) for s in shapes],
            pltpu.SemaphoreType.DMA((5,)),
            pltpu.SemaphoreType.DMA((15,)),
        ],
        compiler_params=pltpu.CompilerParams(vmem_limit_bytes=56 * 2**20),
        cost_estimate=pl.CostEstimate(
            flops=6 * TOKENS * D_LOCAL * H_LOCAL, bytes_accessed=22 * 2**20, transcendentals=0
        ),
        name="weight_grads",
    )(tokens, deltas)


def per_device(activations, out_grad, w_gate, w_up, w_down):
    tokens, deltas, near, other = exchange(activations, out_grad, w_gate, w_up, w_down)
    other = lax.ppermute(other, "col", [(c, (c + 8) % 16) for c in range(16)])
    gate_grad, up_grad, down_grad = weight_grads(tokens, deltas)
    return (near + other).astype(BF16), gate_grad, up_grad, down_grad


def solution(mesh):
    placed = (P("col", "row"), P("col", "row"), P("row", "col"), P("row", "col"), P("col", "row"))
    return jax.shard_map(
        per_device,
        mesh=mesh,
        in_specs=placed,
        out_specs=(P("col", "row"), P("row", "col"), P("row", "col"), P("col", "row")),
        check_vma=False,
    )
```

```python
import functools

import jax
import jax.numpy as jnp
from jax import lax
from jax.experimental import pallas as pl
from jax.experimental.pallas import tpu as pltpu
from jax.sharding import PartitionSpec as P

F32 = jnp.float32
BF16 = jnp.bfloat16
MESH = pl.DeviceIdType.MESH

CHUNKS = 6
CHUNK = 128
OWN = 16
SLOTS = 4
D_LOCAL = 1024
H_LOCAL = 1664
TOKENS = 768
BLOCK = 48
WIDTH_A = 768
HALF_A = 384
WIDTH_B = H_LOCAL - WIDTH_A
LEAD = 32
BLOCK_ORDER = (
    (0, 0), (0, 1), (1, 0), (2, 0), (3, 0), (1, 1), (2, 1), (3, 1),
    (4, 0), (4, 1), (5, 0), (5, 1), (6, 0), (6, 1), (7, 0), (7, 1),
)


def dot_nn(a, b):
    return jnp.dot(a, b, preferred_element_type=F32)


def dot_nt(a, b):
    return lax.dot_general(a, b, (((1,), (1,)), ((), ())), preferred_element_type=F32)


def dot_tn(a, b):
    return lax.dot_general(a, b, (((0,), (0,)), ((), ())), preferred_element_type=F32)


def swiglu_back(gate, upper, hidden_grad):
    sig = jax.nn.sigmoid(gate)
    act = gate * sig
    hidden = (act * upper).astype(BF16)
    gate_delta = (hidden_grad * upper * sig * (1.0 + gate * (1.0 - sig))).astype(BF16)
    up_delta = (hidden_grad * act).astype(BF16)
    return hidden, gate_delta, up_delta


def exchange_kernel(
    act_in, grad_in, wg_in, wu_in, wd_in,
    tokens_out, delta_out, near_out, other_out,
    wg, wu, wd, tok, part_a, part_b,
    send_az, recv_az, send_ay, recv_af, recv_as, recv_ay,
    send_by, recv_bu, recv_by, send_bz, recv_bz,
    delta_a, delta_b, igrad, core_recv, x_recv,
    load_sem, zh_s, zh_r, sib_s, sib_r, tokx_s, tokx_r,
    az_s, az_r, bz_s, bz_r, gaz_s, gaz_r, gbz_s, gbz_r,
    ay_s, ay_r, by_s, by_r, gay_s, gay_r, gby_s, gby_r,
    core_s, core_r, x_s, x_r, out_sem,
):
    row = lax.axis_index("row")
    col = lax.axis_index("col")
    y = lax.rem(row, 4)
    zl = lax.div(row, 4)
    zh = lax.div(col, 8)
    x = lax.rem(lax.div(col, 2), 4)
    core = lax.rem(col, 2)
    y_next, y_prev, y_far = lax.rem(y + 1, 4), lax.rem(y + 3, 4), lax.rem(y + 2, 4)

    def at_x(dist):
        return (row, zh * 8 + lax.rem(x + dist, 4) * 2 + core)

    up_y = (zl * 4 + y_next, col)
    down_y = (zl * 4 + y_prev, col)
    z_pair = ((1 - zl) * 4 + y, col)
    zh_pair = (row, (1 - zh) * 8 + x * 2 + core)
    sibling = (row, zh * 8 + x * 2 + 1 - core)
    partners = [up_y, down_y, z_pair, at_x(1), at_x(2), at_x(3), zh_pair, sibling]

    def remote(src, dst, send, recv, device):
        return pltpu.make_async_remote_copy(
            src_ref=src, dst_ref=dst, send_sem=send, recv_sem=recv,
            device_id=device, device_id_type=MESH,
        )

    unit_dist = (0, 1, 3, 2, 2, 1, 3, 0)
    to_unit = {(0, 3): 1, (0, 1): 2, (0, 2): 3, (1, 2): 4, (1, 3): 5, (1, 1): 6}

    def at(unit, other_core):
        return BLOCK * BLOCK_ORDER.index((unit, other_core))

    def blk(i, unit, other_core):
        return tok.at[i, pl.ds(at(unit, other_core), BLOCK)]

    def to_zh(i):
        return remote(blk(i, 0, 0), blk(i, 7, 0), zh_s.at[i], zh_r.at[i], zh_pair)

    def to_sibling(i, unit):
        return remote(blk(i, unit, 0), blk(i, unit, 1), sib_s.at[i, unit], sib_r.at[i, unit], sibling)

    def to_x(i, other, dist):
        unit = to_unit[other, dist]
        return remote(blk(i, 7 * other, 0), blk(i, unit, 0), tokx_s.at[i, unit - 1], tokx_r.at[i, unit - 1], at_x(dist))

    def pass_on(i, unit):
        if unit == 7:
            to_zh(i).wait_recv()
            for dist in (2, 3, 1):
                to_x(i, 1, dist).start()
        else:
            view = blk(i, unit, 0)
            remote(view, view, tokx_s.at[i, unit - 1], tokx_r.at[i, unit - 1], at_x(unit_dist[unit])).wait_recv()
        to_sibling(i, unit).start()

    again = pl.ds(TOKENS, LEAD)
    loads = [
        pltpu.make_async_copy(act_in, tok.at[0, pl.ds(0, BLOCK)], load_sem.at[0]),
        pltpu.make_async_copy(grad_in, tok.at[1, pl.ds(0, BLOCK)], load_sem.at[1]),
        pltpu.make_async_copy(act_in.at[pl.ds(0, LEAD)], tok.at[0, again], load_sem.at[2]),
        pltpu.make_async_copy(grad_in.at[pl.ds(0, LEAD)], tok.at[1, again], load_sem.at[3]),
        pltpu.make_async_copy(wg_in, wg, load_sem.at[4]),
        pltpu.make_async_copy(wu_in, wu, load_sem.at[5]),
        pltpu.make_async_copy(wd_in, wd, load_sem.at[6]),
    ]
    barrier = pltpu.get_barrier_semaphore()
    for device in partners:
        pl.semaphore_signal(barrier, inc=1, device_id=device, device_id_type=MESH)
    for load in loads:
        load.start()
    pl.semaphore_wait(barrier, len(partners))

    loads[0].wait()
    loads[1].wait()
    for i in range(2):
        to_x(i, 0, 3).start()
        to_x(i, 0, 1).start()
        to_sibling(i, 0).start()
    for i in range(2):
        to_zh(i).start()
        to_x(i, 0, 2).start()

    def first_tokens(i):
        to_sibling(i, 0).wait_recv()
        pass_on(i, 1)
        pass_on(i, 2)

    for load in loads[2:6]:
        load.wait()
    first_tokens(0)

    def rows_a(c, y_):
        return pl.ds(c * CHUNK + 64 * zl + OWN * y_, OWN)

    def rows_b(c, y_, first, size):
        return pl.ds(c * CHUNK + 32 * y_ + first, size)

    first_a, second_a = pl.ds(0, HALF_A), pl.ds(HALF_A, WIDTH_A - HALF_A)

    def send_az_copy(c, i):
        return remote(send_az.at[c, i], recv_az.at[c, i], az_s.at[c, i], az_r.at[c, i], z_pair)

    def send_bz_copy(c):
        return remote(send_bz.at[c], recv_bz.at[c], bz_s.at[c], bz_r.at[c], z_pair)

    def ay(c, k):
        def src(y_, cols):
            return send_ay.at[c, :, pl.ds(OWN * y_, OWN), cols]

        sem = (ay_s.at[c, k], ay_r.at[c, k])
        if k == 0:
            return remote(src(y_far, first_a), recv_af.at[c], *sem, up_y)
        if k == 1:
            return remote(src(y_far, second_a), recv_as.at[c], *sem, down_y)
        if k == 2:
            return remote(src(y_next, second_a), recv_ay.at[c, 0, :, :, second_a], *sem, up_y)
        if k == 3:
            return remote(src(y_prev, first_a), recv_ay.at[c, 1, :, :, first_a], *sem, down_y)
        if k == 4:
            return remote(src(y_next, first_a), recv_ay.at[c, 0, :, :, first_a], *sem, up_y)
        return remote(src(y_prev, second_a), recv_ay.at[c, 1, :, :, second_a], *sem, down_y)

    def by(c, k):
        def src(y_, half):
            return send_by.at[c, :, pl.ds(32 * y_ + OWN * half, OWN)]

        def dst(side, half):
            return recv_by.at[c, side, :, pl.ds(OWN * half, OWN)]

        sem = (by_s.at[c, k], by_r.at[c, k])
        if k == 0:
            return remote(src(y_far, 0), recv_bu.at[c, 0], *sem, up_y)
        if k == 1:
            return remote(src(y_far, 1), recv_bu.at[c, 1], *sem, down_y)
        if k == 2:
            return remote(src(y_next, 1), dst(0, 1), *sem, up_y)
        if k == 3:
            return remote(src(y_prev, 0), dst(1, 0), *sem, down_y)
        if k == 4:
            return remote(src(y_next, 0), dst(0, 0), *sem, up_y)
        return remote(src(y_prev, 1), dst(1, 1), *sem, down_y)

    def same(view, send, recv, device):
        return remote(view, view, send, recv, device)

    def gather_az(c, k, zl_):
        y_ = (y, y_prev, y_next, y_far)[k]
        view = delta_a.at[:, pl.ds(c * CHUNK + 64 * zl_ + OWN * y_, OWN)]
        return same(view, gaz_s.at[c, k], gaz_r.at[c, k], z_pair)

    def gather_bz(c, zl_):
        return same(delta_b.at[:, rows_b(c, y, OWN * zl_, OWN)], gbz_s.at[c], gbz_r.at[c], z_pair)

    def gather_ay(c, k, y_):
        sem = (gay_s.at[c, k], gay_r.at[c, k])
        rows = rows_a(c, y_)
        view = (delta_a.at[:, rows], delta_a.at[:, rows],
                delta_a.at[:, rows, second_a], delta_a.at[:, rows, first_a])[k]
        return same(view, *sem, down_y if k % 2 else up_y)

    def gather_by(c, k, y_):
        sem = (gby_s.at[c, k], gby_r.at[c, k])
        rows = (rows_b(c, y_, 0, 32), rows_b(c, y_, 0, 32), rows_b(c, y_, OWN, OWN), rows_b(c, y_, 0, OWN))[k]
        return same(delta_b.at[:, rows], *sem, down_y if k % 2 else up_y)

    def out_copies(c):
        rows = pl.ds(c * CHUNK, CHUNK)
        return (
            pltpu.make_async_copy(delta_a.at[:, rows], delta_out.at[:, rows, pl.ds(0, WIDTH_A)], out_sem.at[0, c]),
            pltpu.make_async_copy(delta_b.at[:, rows], delta_out.at[:, rows, pl.ds(WIDTH_A, WIDTH_B)], out_sem.at[1, c]),
        )

    tokens_copy = pltpu.make_async_copy(tok.at[:, pl.ds(LEAD, TOKENS)], tokens_out, load_sem.at[0])

    def partial_a(c):
        p = lax.rem(c, SLOTS)
        rows = pl.ds(LEAD + c * CHUNK, CHUNK)

        def send(i):
            send_az[c, i] = part_a[p, i, pl.ds(64 * (1 - zl), 64), :].astype(BF16)
            send_az_copy(c, i).start()

        act = tok[0, rows, :]
        part_a[p, 0] = dot_nn(act, wg[:, :WIDTH_A])
        send(0)
        part_a[p, 1] = dot_nn(act, wu[:, :WIDTH_A])
        send(1)

        @pl.when(c == 0)
        def _():
            loads[6].wait()
            first_tokens(1)

        part_a[p, 2] = dot_nt(tok[1, rows, :], wd[:WIDTH_A, :])
        send(2)

    def partial_b(c):
        p = lax.rem(c, SLOTS)
        rows = pl.ds(LEAD + c * CHUNK, CHUNK)
        act = tok[0, rows, :]
        part_b[p, 0] = dot_nn(act, wg[:, WIDTH_A:])
        part_b[p, 1] = dot_nn(act, wu[:, WIDTH_A:])
        part_b[p, 2] = dot_nt(tok[1, rows, :], wd[WIDTH_A:, :])
        for i in range(3):
            send_by[c, i] = part_b[p, i].astype(BF16)
        for k in range(4):
            by(c, k).start()

    def plane_a(c):
        p = lax.rem(c, SLOTS)
        plane = pl.ds(64 * zl, 64)
        for i in range(3):
            send_az_copy(c, i).wait_recv()
            total = part_a[p, i, plane, :] + recv_az[c, i].astype(F32)
            part_a[p, i, plane, :] = total
            send_ay[c, i] = total.astype(BF16)
        for k in range(4):
            ay(c, k).start()

    def ring_a(c):
        p = lax.rem(c, SLOTS)
        ay(c, 0).wait_recv()
        for i in range(3):
            total = part_a[p, i, pl.ds(64 * zl + OWN * y_next, OWN), :HALF_A] + recv_af[c, i].astype(F32)
            send_ay[c, i, pl.ds(OWN * y_next, OWN), :HALF_A] = total.astype(BF16)
        ay(c, 4).start()
        ay(c, 1).wait_recv()
        for i in range(3):
            total = part_a[p, i, pl.ds(64 * zl + OWN * y_prev, OWN), HALF_A:] + recv_as[c, i].astype(F32)
            send_ay[c, i, pl.ds(OWN * y_prev, OWN), HALF_A:] = total.astype(BF16)
        ay(c, 5).start()

    def ring_b(c):
        p = lax.rem(c, SLOTS)
        for side, y_ in ((0, y_next), (1, y_prev)):
            by(c, side).wait_recv()
            mine = pl.ds(32 * y_ + OWN * side, OWN)
            for i in range(3):
                total = part_b[p, i, mine, :] + recv_bu[c, side, i].astype(F32)
                send_by[c, i, mine, :] = total.astype(BF16)
            by(c, 4 + side).start()

    def own_a(c):
        p = lax.rem(c, SLOTS)
        for k in range(2, 6):
            ay(c, k).wait_recv()
        mine = pl.ds(64 * zl + OWN * y, OWN)
        sums = [
            part_a[p, i, mine, :] + recv_ay[c, 0, i].astype(F32) + recv_ay[c, 1, i].astype(F32)
            for i in range(3)
        ]
        for i, value in enumerate(swiglu_back(*sums)):
            delta_a[i, rows_a(c, y), :] = value
        gather_az(c, 0, zl).start()
        for k in range(2):
            gather_ay(c, k, y).start()

    def own_b(c):
        p = lax.rem(c, SLOTS)
        for k in range(2, 6):
            by(c, k).wait_recv()
        for half in range(2):
            mine = pl.ds(32 * y + OWN * half, OWN)
            for i in range(3):
                total = part_b[p, i, mine, :]
                for side in range(2):
                    total = total + recv_by[c, side, i, pl.ds(OWN * half, OWN), :].astype(F32)
                part_b[p, i, mine, :] = total
        for i in range(3):
            send_bz[c, i] = part_b[p, i, pl.ds(32 * y + OWN * (1 - zl), OWN), :].astype(BF16)
        send_bz_copy(c).start()

    def point_b(c):
        p = lax.rem(c, SLOTS)
        send_bz_copy(c).wait_recv()
        mine = pl.ds(32 * y + OWN * zl, OWN)
        sums = [part_b[p, i, mine, :] + recv_bz[c, i].astype(F32) for i in range(3)]
        for i, value in enumerate(swiglu_back(*sums)):
            delta_b[i, rows_b(c, y, OWN * zl, OWN), :] = value
        gather_bz(c, zl).start()

    def forward_a(c):
        gather_ay(c, 0, y_prev).wait_recv()
        gather_ay(c, 2, y_prev).start()
        gather_az(c, 1, zl).start()
        gather_ay(c, 1, y_next).wait_recv()
        gather_ay(c, 3, y_next).start()
        gather_az(c, 2, zl).start()

    def quarter_b(c):
        gather_bz(c, 1 - zl).wait_recv()
        for k in range(2):
            gather_by(c, k, y).start()

    def swap_a(c):
        for k in (2, 3):
            gather_ay(c, k, y_far).wait_recv()
        gather_az(c, 3, zl).start()

    def forward_b(c):
        gather_by(c, 0, y_prev).wait_recv()
        gather_by(c, 2, y_prev).start()
        gather_by(c, 1, y_next).wait_recv()
        gather_by(c, 3, y_next).start()

    def input_grad_a(c):
        rows, out = pl.ds(c * CHUNK, CHUNK), pl.ds(LEAD + c * CHUNK, CHUNK)
        for k in range(4):
            gather_az(c, k, 1 - zl).wait_recv()
        igrad[out, :] = dot_nt(delta_a[1, rows, :], wg[:, :WIDTH_A])
        igrad[out, :] += dot_nt(delta_a[2, rows, :], wu[:, :WIDTH_A])

    def input_grad_b(c):
        rows, out = pl.ds(c * CHUNK, CHUNK), pl.ds(LEAD + c * CHUNK, CHUNK)
        for k in (2, 3):
            gather_by(c, k, y_far).wait_recv()
        for copy in out_copies(c):
            copy.start()
        igrad[out, :] += dot_nt(delta_b[1, rows, :], wg[:, WIDTH_A:])
        igrad[out, :] += dot_nt(delta_b[2, rows, :], wu[:, WIDTH_A:])

    def core_copy(unit):
        src = igrad.at[pl.ds(at(unit, 1), BLOCK)]
        return remote(src, core_recv.at[unit], core_s.at[unit], core_r.at[unit], sibling)

    def x_copy(unit):
        src = igrad.at[pl.ds(at(unit, 0), BLOCK)]
        return remote(src, x_recv.at[unit - 1], x_s.at[unit - 1], x_r.at[unit - 1], at_x(unit_dist[unit]))

    def sum_core(unit):
        core_copy(unit).wait_recv()
        rows = pl.ds(at(unit, 0), BLOCK)
        igrad[rows, :] = igrad[rows, :] + core_recv[unit]
        x_copy(unit).start()

    stages = (
        (6, input_grad_a), (6, input_grad_b), (5, swap_a), (5, forward_b), (4, forward_a), (4, quarter_b),
        (3, own_a), (3, point_b), (2, ring_a), (2, own_b), (1, plane_a), (1, ring_b), (0, partial_a), (0, partial_b),
    )
    units_done = ((0,), (1,), (2, 3), (4,), (5, 6), (7,))
    units_wait = ((), (1,), (2, 3), (4, 5), (6,), (7,))
    units_pass = ((3, 7), (4, 5), (6,))

    first = [stage for delay, stage in stages if delay == 0][0]
    last = max(delay for delay, _ in stages)

    @pl.loop(0, CHUNKS + last)
    def _(t):
        for delay, stage in stages:
            if stage is first:
                for c in range(1, CHUNKS):
                    @pl.when(t == c)
                    def _():
                        for unit in units_wait[c]:
                            for i in range(2):
                                to_sibling(i, unit).wait_recv()

            if stage is input_grad_a:
                for c in range(CHUNKS - 1):
                    @pl.when(t == c + last + 1)
                    def _():
                        for unit in units_done[c]:
                            if unit:
                                sum_core(unit)

            @pl.when((t >= delay) & (t < CHUNKS + delay))
            def _():
                stage(t - delay)

            if stage is input_grad_b:
                for c in range(CHUNKS):
                    @pl.when(t == c + last)
                    def _():
                        for unit in units_done[c]:
                            core_copy(unit).start()

        for c, units in enumerate(units_pass):
            @pl.when(t == c)
            def _():
                for unit in units:
                    for i in range(2):
                        pass_on(i, unit)

        @pl.when(t == CHUNKS - 1)
        def _():
            tokens_copy.start()

    core_copy(0).wait_recv()
    near = igrad[pl.ds(at(0, 0) + LEAD, BLOCK - LEAD), :], igrad[again, :]
    near = jnp.concatenate([near[1], near[0]], axis=0) + core_recv[0]
    for unit in (1, 2, 3):
        x_copy(unit).wait_recv()
        near = near + x_recv[unit - 1]
    near_out[...] = near
    core_copy(7).wait_recv()
    other = igrad[pl.ds(at(7, 0), BLOCK), :] + core_recv[7]
    for unit in (4, 5, 6):
        x_copy(unit).wait_recv()
        other = other + x_recv[unit - 1]
    other_out[...] = other

    for i in range(2):
        to_zh(i).wait_send()
        for other_, dist in to_unit:
            to_x(i, other_, dist).wait_send()
        for unit in range(8):
            to_sibling(i, unit).wait_send()
    for unit in range(8):
        core_copy(unit).wait_send()
    for unit in range(1, 7):
        x_copy(unit).wait_send()

    @pl.loop(0, CHUNKS)
    def _(c):
        for i in range(3):
            send_az_copy(c, i).wait_send()
        send_bz_copy(c).wait_send()
        for k in range(4):
            gather_az(c, k, zl).wait_send()
        gather_bz(c, zl).wait_send()
        for k in range(6):
            ay(c, k).wait_send()
            by(c, k).wait_send()
        for k in range(4):
            gather_ay(c, k, y).wait_send()
            gather_by(c, k, y).wait_send()
        for copy in out_copies(c):
            copy.wait()

    tokens_copy.wait()


def exchange(activations, out_grad, w_gate, w_up, w_down):
    dma = pltpu.SemaphoreType.DMA
    any_spec = pl.BlockSpec(memory_space=pl.ANY)
    vmem_spec = pl.BlockSpec(memory_space=pltpu.VMEM)
    n = CHUNKS
    return pl.pallas_call(
        exchange_kernel,
        out_shape=[
            jax.ShapeDtypeStruct((2, TOKENS, D_LOCAL), BF16),
            jax.ShapeDtypeStruct((3, TOKENS, H_LOCAL), BF16),
            *[jax.ShapeDtypeStruct((BLOCK, D_LOCAL), F32)] * 2,
        ],
        in_specs=[any_spec] * 5,
        out_specs=[any_spec] * 2 + [vmem_spec] * 2,
        scratch_shapes=[
            pltpu.VMEM((D_LOCAL, H_LOCAL), BF16),
            pltpu.VMEM((D_LOCAL, H_LOCAL), BF16),
            pltpu.VMEM((H_LOCAL, D_LOCAL), BF16),
            pltpu.VMEM((2, TOKENS + LEAD, D_LOCAL), BF16),
            pltpu.VMEM((SLOTS, 3, CHUNK, WIDTH_A), F32),
            pltpu.VMEM((SLOTS, 3, CHUNK, WIDTH_B), F32),
            pltpu.VMEM((n, 3, 64, WIDTH_A), BF16),
            pltpu.VMEM((n, 3, 64, WIDTH_A), BF16),
            pltpu.VMEM((n, 3, 64, WIDTH_A), BF16),
            pltpu.VMEM((n, 3, OWN, HALF_A), BF16),
            pltpu.VMEM((n, 3, OWN, WIDTH_A - HALF_A), BF16),
            pltpu.VMEM((n, 2, 3, OWN, WIDTH_A), BF16),
            pltpu.VMEM((n, 3, CHUNK, WIDTH_B), BF16),
            pltpu.VMEM((n, 2, 3, OWN, WIDTH_B), BF16),
            pltpu.VMEM((n, 2, 3, 32, WIDTH_B), BF16),
            pltpu.VMEM((n, 3, OWN, WIDTH_B), BF16),
            pltpu.VMEM((n, 3, OWN, WIDTH_B), BF16),
            pltpu.VMEM((3, TOKENS, WIDTH_A), BF16),
            pltpu.VMEM((3, TOKENS, WIDTH_B), BF16),
            pltpu.VMEM((TOKENS + LEAD, D_LOCAL), F32),
            pltpu.VMEM((8, BLOCK, D_LOCAL), F32),
            pltpu.VMEM((6, BLOCK, D_LOCAL), F32),
            dma((7,)), dma((2,)), dma((2,)), dma((2, 8)), dma((2, 8)), dma((2, 6)), dma((2, 6)),
            dma((n, 3)), dma((n, 3)), dma((n,)), dma((n,)), dma((n, 4)), dma((n, 4)), dma((n,)), dma((n,)),
            dma((n, 6)), dma((n, 6)), dma((n, 6)), dma((n, 6)),
            dma((n, 4)), dma((n, 4)), dma((n, 4)), dma((n, 4)),
            dma((8,)), dma((8,)), dma((6,)), dma((6,)),
            dma((2, n)),
        ],
        compiler_params=pltpu.CompilerParams(
            collective_id=0, has_side_effects=True, vmem_limit_bytes=60 * 2**20
        ),
        cost_estimate=pl.CostEstimate(
            flops=10 * TOKENS * D_LOCAL * H_LOCAL, bytes_accessed=22 * 2**20, transcendentals=0
        ),
        name="exchange",
    )(activations, out_grad, w_gate, w_up, w_down)


def weights_kernel(
    tok_in, delta_in, gate_out, up_out, down_out,
    tok, delta, gate, up, down, in_sem, out_sem,
):
    loads = [
        pltpu.make_async_copy(tok_in.at[0], tok.at[0], in_sem.at[0]),
        pltpu.make_async_copy(delta_in.at[1], delta.at[1], in_sem.at[1]),
        pltpu.make_async_copy(delta_in.at[2], delta.at[2], in_sem.at[2]),
        pltpu.make_async_copy(delta_in.at[0], delta.at[0], in_sem.at[3]),
        pltpu.make_async_copy(tok_in.at[1], tok.at[1], in_sem.at[4]),
    ]
    for load in loads:
        load.start()
    stores = []

    def store(src, dst, start, size):
        copy = pltpu.make_async_copy(
            src.at[pl.ds(start, size)], dst.at[pl.ds(start, size)], out_sem.at[len(stores)]
        )
        copy.start()
        stores.append(copy)

    loads[0].wait()
    for load, i, buf, out in ((loads[1], 1, gate, gate_out), (loads[2], 2, up, up_out)):
        load.wait()
        for m in range(0, D_LOCAL, 256):
            buf[m : m + 256, :] = dot_tn(tok[0, :, m : m + 256], delta[i]).astype(BF16)
            store(buf, out, m, 256)
    loads[3].wait()
    loads[4].wait()
    for m in range(0, H_LOCAL, 256):
        size = min(256, H_LOCAL - m)
        down[m : m + size, :] = dot_tn(delta[0, :, m : m + size], tok[1]).astype(BF16)
        store(down, down_out, m, size)
    for copy in stores:
        copy.wait()


def weight_grads(tokens, deltas):
    any_spec = pl.BlockSpec(memory_space=pl.ANY)
    shapes = [(D_LOCAL, H_LOCAL), (D_LOCAL, H_LOCAL), (H_LOCAL, D_LOCAL)]
    return pl.pallas_call(
        weights_kernel,
        out_shape=[jax.ShapeDtypeStruct(s, BF16) for s in shapes],
        in_specs=[any_spec] * 2,
        out_specs=[any_spec] * 3,
        scratch_shapes=[
            pltpu.VMEM((2, TOKENS, D_LOCAL), BF16),
            pltpu.VMEM((3, TOKENS, H_LOCAL), BF16),
            *[pltpu.VMEM(s, BF16) for s in shapes],
            pltpu.SemaphoreType.DMA((5,)),
            pltpu.SemaphoreType.DMA((15,)),
        ],
        compiler_params=pltpu.CompilerParams(vmem_limit_bytes=56 * 2**20),
        cost_estimate=pl.CostEstimate(
            flops=6 * TOKENS * D_LOCAL * H_LOCAL, bytes_accessed=22 * 2**20, transcendentals=0
        ),
        name="weight_grads",
    )(tokens, deltas)


def per_device(activations, out_grad, w_gate, w_up, w_down):
    tokens, deltas, near, other = exchange(activations, out_grad, w_gate, w_up, w_down)
    other = lax.ppermute(other, "col", [(c, (c + 8) % 16) for c in range(16)])
    gate_grad, up_grad, down_grad = weight_grads(tokens, deltas)
    return (near + other).astype(BF16), gate_grad, up_grad, down_grad


def solution(mesh):
    placed = (P("col", "row"), P("col", "row"), P("row", "col"), P("row", "col"), P("col", "row"))
    return jax.shard_map(
        per_device,
        mesh=mesh,
        in_specs=placed,
        out_specs=(P("col", "row"), P("row", "col"), P("row", "col"), P("col", "row")),
        check_vma=False,
    )
```
